32 devices in a mesh: row: 4 (over z), col: 2 (over y), layer: 4 (over x, core).
Axes of the slice: x: 2, y: 2, z: 4, core: 2. Of those that a mesh axis runs over, the one named last changes fastest.
Arguments:
- left_blocks: bfloat16 [4096, 16384], P('row', ('layer', 'col')), may hold values from -6 to 6
- left_pattern: int32 [64, 256], P('row', ('layer', 'col')), may hold values 0 or 1
- right_blocks: bfloat16 [16384, 2048], P(('layer', 'col'), 'row'), may hold values from -0.125 to 0.125
- right_pattern: int32 [256, 32], P(('layer', 'col'), 'row'), may hold values 0 or 1
Outputs:
- product: bfloat16 [4096, 2048], P('row', ('col', 'layer'))
The draws below stay inside these ranges and needn't reach their ends.
All inputs are finite; a program needn't handle non-finite values. No bound on the sum of `left_pattern` or of `right_pattern` on one device may be relied on, other than what follows from the above.
Results may differ from the reference program's by a relative error of at most 0.001.
Values may be sent and summed in bfloat16 or wider, within the bound.
A program may use at most 64 MiB of HBM per device.

```python
import jax
import jax.numpy as jnp

BS = 64
M = 4096
K = 16384
N = 2048


def set_ends(array, own_key, low, largest):
    place = [jax.random.randint(jax.random.fold_in(own_key, axis), (), 0, length) for axis, length in enumerate(array.shape)]
    widest = array.shape.index(max(array.shape))
    neighbour = place[:widest] + [(place[widest] + 1) % array.shape[widest]] + place[widest + 1:]
    return array.at[tuple(place)].set(low).at[tuple(neighbour)].set(largest)


def with_spikes(drawn, key, source, target, blocks, factor):
    owner, partner = [(jnp.arange(drawn.shape[position]) // (drawn.shape[position] // blocks)).reshape([-1 if axis == position else 1 for axis in range(drawn.ndim)]) for position in (source, target)]
    chosen = jax.random.permutation(key, blocks)[partner]
    strong = (owner == chosen) | (owner == (partner + blocks // 2) % blocks)
    return jnp.where(strong, factor * drawn, drawn)


def block_levels(stream_key, extent, pieces, least, top_value):
    factor_of = 1.0
    for position, blocks in pieces:
        heights = jax.random.uniform(jax.random.fold_in(jax.random.fold_in(stream_key, 6), position), (blocks,), jnp.float32, least / len(pieces), top_value / len(pieces))
        factor_of = factor_of * jnp.repeat(jnp.exp(heights), extent[position] // blocks).reshape((-1,) + (1,) * (len(extent) - 1 - position))
    return factor_of


def gaussian(stream_key, shape, deviation, most, shards=(), held_as=jnp.bfloat16):
    level = block_levels(stream_key, shape, shards, -0.22, 0.18) if shards else 1.0
    entries = jax.random.normal(stream_key, shape, jnp.float32) * deviation * level
    return jnp.minimum(jnp.maximum(entries, -most), most).astype(held_as)


def bell_draw_with(own_key, dims, width, limit, split, heavy, dtype=jnp.bfloat16):
    values = width * jax.random.normal(own_key, dims, jnp.float32)
    if split:
        values = values * block_levels(own_key, dims, split, -0.22, 0.18)
    return jnp.clip(with_spikes(values, jax.random.fold_in(own_key, 3), *heavy), -limit, limit).astype(dtype)


def setup_inputs(seed: int = 0) -> dict:
    keys = jax.random.split(jax.random.key(seed), 5)
    return {
        "left_blocks": gaussian(keys[0], (M, K), 1.0, 6.0, ((0, 4), (1, 8))),
        "left_pattern": set_ends((jax.random.randint(keys[1], (M // BS, K // BS), 0, 2) < 1).astype(jnp.int32), jax.random.fold_in(keys[1], 1), 0, 1),
        "right_blocks": bell_draw_with(keys[2], (K, N), (K // 4) ** -0.5, 0.125, ((0, 8), (1, 4)), (0, 1, 8, 2.0)),
        "right_pattern": set_ends((jax.random.randint(keys[3], (K // BS, N // BS), 0, 2) < 1).astype(jnp.int32), jax.random.fold_in(keys[3], 1), 0, 1),
    }


def apply_pattern(values, pattern):
    rows, cols = values.shape
    shaped = values.reshape(rows // BS, BS, cols // BS, BS)
    masked = shaped * pattern[:, None, :, None].astype(jnp.bfloat16)
    return masked.reshape(rows, cols)


def reference(left_blocks, left_pattern, right_blocks, right_pattern):
    left = apply_pattern(left_blocks, left_pattern)
    right = apply_pattern(right_blocks, right_pattern)
    return jnp.dot(left, right, preferred_element_type=jnp.float32).astype(jnp.bfloat16)
```

```python
import functools

import jax
import jax.numpy as jnp
from jax import lax
from jax.experimental import pallas as pl
from jax.experimental.pallas import tpu as pltpu
from jax.sharding import PartitionSpec as P

MESH = pl.DeviceIdType.MESH
BLOCK = 64
CHUNKS = 4
CAPS = (160, 256)


def from_behind(x, axis, by):
    size = lax.axis_size(axis)
    return lax.ppermute(x, axis, [(i, (i + by) % size) for i in range(size)])


def apply_pattern(values, pattern):
    rows, cols = values.shape
    block = rows // pattern.shape[0]
    shaped = values.reshape(pattern.shape[0], block, pattern.shape[1], block)
    masked = shaped * pattern[:, None, :, None].astype(jnp.bfloat16)
    return masked.reshape(rows, cols)


def local_general(left_blocks, left_pattern, right_blocks, right_pattern):
    left = apply_pattern(left_blocks, left_pattern)
    right = apply_pattern(right_blocks, right_pattern)
    left_rows = left.shape[0]
    range_cols = right.shape[1]
    cycle_size = lax.axis_size("row")
    position = lax.axis_index("row")
    partial_value = jnp.zeros((left_rows, range_cols * cycle_size), jnp.float32)
    current = right
    for step in range(cycle_size):
        if step > 0:
            current = from_behind(current, "row", 1)
        owner = (position - step) % cycle_size
        piece = jnp.dot(left, current, preferred_element_type=jnp.float32)
        partial_value = lax.dynamic_update_slice_in_dim(partial_value, piece, owner * range_cols, 1)
    reduced = lax.psum_scatter(partial_value, ("col", "layer"), scatter_dimension=1, tiled=True)
    return reduced.astype(jnp.bfloat16)


def turn(tile):
    return jnp.concatenate([tile[:, BLOCK:], tile[:, :BLOCK]], axis=1)


def join(a, b, stay_a, turn_a, stay_b, turn_b):
    left = jnp.where(lax.broadcasted_iota(jnp.int32, (1, 128), 1) < BLOCK, 1.0, 0.0)
    right = 1.0 - left
    first = a * (left * stay_a).astype(jnp.bfloat16) + turn(a) * (left * turn_a).astype(jnp.bfloat16)
    second = b * (right * stay_b).astype(jnp.bfloat16) + turn(b) * (right * turn_b).astype(jnp.bfloat16)
    return first + second


def kernel(cap, left_ref, lpat_ref, right_ref, tile_ref, stay_ref, turn_ref, from_ref, keep_ref, flip_ref, out_ref,
           masked, tiled, held, current, wide, part, swapped, got, done,
           zsend, zrecv, xsend, xrecv, rsend, rrecv, fsend, frecv):
    z = lax.axis_index("row")
    col = lax.axis_index("col")
    layer = lax.axis_index("layer")
    core = lax.rem(layer, 2)
    chip = col * 2 + lax.div(layer, 2)
    tiles = cap // 2 // CHUNKS
    rows, width = left_ref.shape[0], right_ref.shape[1]
    quarter = rows // 4
    half = width // 2
    kblocks = right_ref.shape[0] // BLOCK
    strips = width // 128

    def at_chip(q):
        return (z, lax.div(q, 2), lax.rem(q, 2) * 2 + core)

    partner = (z, col, lax.div(layer, 2) * 2 + 1 - core)
    above, below = (z + 1, col, layer), (z - 1, col, layer)
    has_above, has_below = z < 3, z > 0

    barrier = pltpu.get_barrier_semaphore()

    @pl.when(has_above)
    def _():
        pl.semaphore_signal(barrier, inc=1, device_id=above, device_id_type=MESH)

    @pl.when(has_below)
    def _():
        pl.semaphore_signal(barrier, inc=1, device_id=below, device_id_type=MESH)

    pl.semaphore_signal(barrier, inc=1, device_id=partner, device_id_type=MESH)
    for i in range(1, 4):
        pl.semaphore_signal(barrier, inc=1, device_id=at_chip(lax.rem(chip + i, 4)), device_id_type=MESH)
    pl.semaphore_wait(barrier, 4 + jnp.where(has_above, 1, 0) + jnp.where(has_below, 1, 0))

    def up(j, c):
        piece = held.at[j, pl.ds(c * tiles, tiles)]
        return pltpu.make_async_remote_copy(
            src_ref=piece, dst_ref=piece, send_sem=zsend.at[0, j, c], recv_sem=zrecv.at[j, c],
            device_id=above, device_id_type=MESH)

    def down(j, c):
        piece = held.at[j, pl.ds(c * tiles, tiles)]
        return pltpu.make_async_remote_copy(
            src_ref=piece, dst_ref=piece, send_sem=zsend.at[1, j, c], recv_sem=zrecv.at[j, c],
            device_id=below, device_id_type=MESH)

    def pack(c):
        def one(t, carry):
            e, o = 2 * t, 2 * t + 1
            held[z, t] = join(tiled[from_ref[e]], tiled[from_ref[o]],
                              keep_ref[e], flip_ref[e], keep_ref[o], flip_ref[o])
            return carry
        lax.fori_loop(c * tiles, (c + 1) * tiles, one, 0)

    def cut(k, carry):
        for m in range(strips):
            tiled[k * strips + m] = right_ref[pl.ds(pl.multiple_of(k * BLOCK, BLOCK), BLOCK), m * 128:(m + 1) * 128]
        return carry

    lax.fori_loop(0, kblocks, cut, 0)
    for c in range(CHUNKS):
        pack(c)

        @pl.when(has_above)
        def _():
            up(z, c).start()

        @pl.when(has_below)
        def _():
            down(z, c).start()

    depth = left_ref.shape[1]
    spread = (lax.broadcasted_iota(jnp.int32, (depth // BLOCK, depth), 1) // BLOCK
              == lax.broadcasted_iota(jnp.int32, (depth // BLOCK, depth), 0))
    lmask = jnp.dot(lpat_ref[...].astype(jnp.float32), jnp.where(spread, 1.0, 0.0),
                    preferred_element_type=jnp.float32)
    for i in range(rows // BLOCK):
        masked[i * BLOCK:(i + 1) * BLOCK, :] = (
            left_ref[i * BLOCK:(i + 1) * BLOCK, :] * lmask[i:i + 1, :].astype(jnp.bfloat16))

    def order(r):
        if r == 0:
            return z
        y = jnp.where(z < 2, z, 3 - z)
        o = {1: y + 1, 2: 2 - 2 * y, 3: 3 + 0 * y}[r]
        return jnp.where(z < 2, o, 3 - o)

    def step(t):
        away, c = t // CHUNKS + 1, t % CHUNKS

        @pl.when(z + away <= 3)
        def _():
            j = z + away
            down(j, c).wait_recv()

            @pl.when(has_below)
            def _():
                down(j, c).start()

        @pl.when(z - away >= 0)
        def _():
            j = z - away
            up(j, c).wait_recv()

            @pl.when(has_above)
            def _():
                up(j, c).start()

    def expand(r):
        j = order(r)

        def fetch(t, carry):
            current[t] = held[j, t]
            return carry
        lax.fori_loop(0, cap // 2, fetch, 0)

        def one(k, carry):
            for m in range(strips):
                e = (j * kblocks + k) * (2 * strips) + 2 * m
                o = e + 1
                wide[pl.ds(pl.multiple_of(k * BLOCK, BLOCK), BLOCK), m * 128:(m + 1) * 128] = join(
                    current[tile_ref[e]], current[tile_ref[o]],
                    stay_ref[e], turn_ref[e], stay_ref[o], turn_ref[o])
            return carry
        lax.fori_loop(0, kblocks, one, 0)

    def swap(r, q):
        return pltpu.make_async_remote_copy(
            src_ref=part.at[r, 1 - core, q], dst_ref=swapped.at[r, q],
            send_sem=xsend.at[r, q], recv_sem=xrecv.at[r, q],
            device_id=partner, device_id_type=MESH)

    def multiply(r):
        def one(i, carry):
            q = lax.rem(chip + 1 + i, 4)
            piece = jnp.dot(masked[pl.ds(pl.multiple_of(q * quarter, quarter), quarter), :], wide[...],
                            preferred_element_type=jnp.float32)
            part[r, 0, q] = piece[:, :half]
            part[r, 1, q] = piece[:, half:]
            swap(r, q).start()
            return carry
        lax.fori_loop(0, 4, one, 0)

    def scatter(r, i):
        q = lax.rem(chip + i, 4)
        return pltpu.make_async_remote_copy(
            src_ref=part.at[r, core, q], dst_ref=got.at[r, 3 - i],
            send_sem=rsend.at[r, i - 1], recv_sem=rrecv.at[r, 3 - i],
            device_id=at_chip(q), device_id_type=MESH)

    def arrival(r, i):
        return pltpu.make_async_remote_copy(
            src_ref=part.at[r, core, chip], dst_ref=got.at[r, i - 1],
            send_sem=rsend.at[r, i - 1], recv_sem=rrecv.at[r, i - 1],
            device_id=at_chip(lax.rem(chip + i, 4)), device_id_type=MESH)

    def add_cores(r):
        for i in range(1, 5):
            q = lax.rem(chip + i, 4)
            swap(r, q).wait_recv()
            part[r, core, q] = part[r, core, q] + swapped[r, q]
            if i < 4:
                scatter(r, i).start()

    def finish(r):
        j = order(r)
        mine = pl.ds(pl.multiple_of(chip * quarter, quarter), quarter)
        for i in range(1, 4):
            arrival(r, i).wait_recv()
        total = (part[r, core, chip] + got[r, 0]) + (got[r, 1] + got[r, 2])

        @pl.when(j == chip)
        def _():
            out_ref[mine, :] = total.astype(jnp.bfloat16)

        @pl.when(j != chip)
        def _():
            done[r] = total.astype(jnp.bfloat16)
            deliver(r, j, chip).start()

    def deliver(r, to, source):
        rng = pl.ds(pl.multiple_of(source * quarter, quarter), quarter)
        return pltpu.make_async_remote_copy(
            src_ref=done.at[r], dst_ref=out_ref.at[rng], send_sem=fsend.at[r], recv_sem=frecv.at[source],
            device_id=at_chip(to), device_id_type=MESH)

    for r in range(4):
        if r > 0:
            step((r - 1) * CHUNKS + CHUNKS - 1)
        expand(r)
        if r < 3:
            step(r * CHUNKS)
        multiply(r)
        if r < 3:
            step(r * CHUNKS + 1)
        add_cores(r)
        if r < 3:
            step(r * CHUNKS + 2)
        finish(r)

    for i in range(1, 4):
        q = lax.rem(chip + i, 4)
        deliver(0, q, q).wait_recv()
    for r in range(4):
        @pl.when(order(r) != chip)
        def _():
            deliver(r, order(r), chip).wait_send()
        for q in range(4):
            swap(r, q).wait_send()
        for i in range(1, 4):
            scatter(r, i).wait_send()
    for j in range(4):
        for c in range(CHUNKS):
            @pl.when(has_above & (j <= z))
            def _():
                up(j, c).wait_send()

            @pl.when(has_below & (j >= z))
            def _():
                down(j, c).wait_send()


def run(cap, index, left, lpat, right, present, slot, inv):
    rows, width = left.shape[0], right.shape[1]
    quarter, half = rows // 4, width // 2
    dma = pltpu.SemaphoreType.DMA
    vmem = pl.BlockSpec(memory_space=pltpu.VMEM)
    smem = pl.BlockSpec(memory_space=pltpu.SMEM)
    side = jnp.arange(slot.size, dtype=jnp.int32) % 2
    same = (slot % 2 == side).astype(jnp.float32)
    there = present.astype(jnp.float32)
    tile = jnp.minimum(slot // 2, cap // 2 - 1)
    keep = (inv % 2 == jnp.arange(inv.size, dtype=jnp.int32) % 2).astype(jnp.float32)
    tiles = (right.shape[0] // BLOCK) * (width // 128)
    return pl.pallas_call(
        functools.partial(kernel, cap),
        out_shape=jax.ShapeDtypeStruct((rows, half), jnp.bfloat16),
        in_specs=[vmem, vmem, vmem] + [smem] * 6,
        out_specs=vmem,
        scratch_shapes=[
            pltpu.VMEM(left.shape, jnp.bfloat16),
            pltpu.VMEM((tiles, BLOCK, 128), jnp.bfloat16),
            pltpu.VMEM((4, cap // 2, BLOCK, 128), jnp.bfloat16),
            pltpu.VMEM((cap // 2, BLOCK, 128), jnp.bfloat16),
            pltpu.VMEM(right.shape, jnp.bfloat16),
            pltpu.VMEM((4, 2, 4, quarter, half), jnp.float32),
            pltpu.VMEM((4, 4, quarter, half), jnp.float32),
            pltpu.VMEM((4, 3, quarter, half), jnp.float32),
            pltpu.VMEM((4, quarter, half), jnp.bfloat16),
            dma((2, 4, CHUNKS)), dma((4, CHUNKS)),
            dma((4, 4)), dma((4, 4)), dma((4, 3)), dma((4, 3)), dma((4,)), dma((4,)),
        ],
        compiler_params=pltpu.CompilerParams(
            collective_id=index, has_side_effects=True, vmem_limit_bytes=56 * 2**20),
        name=f"sparse_product_{cap}",
    )(left, lpat, right, tile, there * same, there * (1 - same), inv // 2, keep, 1 - keep)


def local_packed(left, lpat, right, rpat):
    every = lax.all_gather(rpat, ("layer", "col", "row"), axis=0, tiled=False)
    everyone = every.reshape(-1, 4, rpat.size)
    most = jnp.max(jnp.sum(everyone, axis=2))
    group = lax.axis_index("layer") * lax.axis_size("col") + lax.axis_index("col")
    present = lax.dynamic_index_in_dim(everyone, group, 0, keepdims=False)
    slot = jnp.cumsum(present, axis=1) - present
    own = rpat.reshape(-1)
    place = jnp.cumsum(own) - own
    index = jnp.arange(own.size, dtype=jnp.int32)
    hit = (place[None, :] == index[:, None]) & (own[None, :] > 0)
    inv = jnp.sum(jnp.where(hit, index[None, :], 0), axis=1)
    which = sum((most > cap).astype(jnp.int32) for cap in CAPS[:-1])
    return lax.switch(
        which, [functools.partial(run, cap, i) for i, cap in enumerate(CAPS)],
        left, lpat, right, present.reshape(-1), slot.reshape(-1), inv)


def solution(mesh):
    placed = (
        P("row", ("layer", "col")),
        P("row", ("layer", "col")),
        P(("layer", "col"), "row"),
        P(("layer", "col"), "row"),
    )
    sizes = tuple(mesh.shape[axis] for axis in ("row", "col", "layer"))
    local = local_packed if sizes == (4, 2, 4) else local_general
    return jax.shard_map(
        local, mesh=mesh, in_specs=placed, out_specs=P("row", ("col", "layer")), check_vma=False
    )
```

```python
import functools

import jax
import jax.numpy as jnp
from jax import lax
from jax.experimental import pallas as pl
from jax.experimental.pallas import tpu as pltpu
from jax.sharding import PartitionSpec as P

MESH = pl.DeviceIdType.MESH
BLOCK = 64
CAP = 160
CHUNKS = 8
READY = (3, 5, 7, 8)


def from_behind(x, axis, by):
    size = lax.axis_size(axis)
    return lax.ppermute(x, axis, [(i, (i + by) % size) for i in range(size)])


def apply_pattern(values, pattern):
    rows, cols = values.shape
    block = rows // pattern.shape[0]
    shaped = values.reshape(pattern.shape[0], block, pattern.shape[1], block)
    masked = shaped * pattern[:, None, :, None].astype(jnp.bfloat16)
    return masked.reshape(rows, cols)


def local_general(left_blocks, left_pattern, right_blocks, right_pattern):
    left = apply_pattern(left_blocks, left_pattern)
    right = apply_pattern(right_blocks, right_pattern)
    left_rows = left.shape[0]
    range_cols = right.shape[1]
    cycle_size = lax.axis_size("row")
    position = lax.axis_index("row")
    partial_value = jnp.zeros((left_rows, range_cols * cycle_size), jnp.float32)
    current = right
    for step in range(cycle_size):
        if step > 0:
            current = from_behind(current, "row", 1)
        owner = (position - step) % cycle_size
        piece = jnp.dot(left, current, preferred_element_type=jnp.float32)
        partial_value = lax.dynamic_update_slice_in_dim(partial_value, piece, owner * range_cols, 1)
    reduced = lax.psum_scatter(partial_value, ("col", "layer"), scatter_dimension=1, tiled=True)
    return reduced.astype(jnp.bfloat16)


def turn(tile):
    return jnp.concatenate([tile[:, BLOCK:], tile[:, :BLOCK]], axis=1)


def join(a, b, stay_a, turn_a, stay_b, turn_b):
    left = jnp.where(lax.broadcasted_iota(jnp.int32, (1, 128), 1) < BLOCK, 1.0, 0.0)
    right = 1.0 - left
    first = a * (left * stay_a).astype(jnp.bfloat16) + turn(a) * (left * turn_a).astype(jnp.bfloat16)
    second = b * (right * stay_b).astype(jnp.bfloat16) + turn(b) * (right * turn_b).astype(jnp.bfloat16)
    return first + second


def kernel(left_ref, lpat_ref, right_ref, code_ref, pack_ref, out_ref, flag_ref,
           masked, tiled, held, current, wide, part, swapped, got, done, codes, scalars, flags,
           zsend, zrecv, xsend, xrecv, rsend, rrecv, fsend, frecv, csend, crecv, ssem, gsend, grecv):
    z = lax.axis_index("row")
    col = lax.axis_index("col")
    layer = lax.axis_index("layer")
    core = lax.rem(layer, 2)
    chip = col * 2 + lax.div(layer, 2)
    tiles = CAP // 2 // CHUNKS
    rows = left_ref.shape[0]
    quarter, eighth = rows // 4, rows // 8
    kblocks = right_ref.shape[0] // BLOCK
    strips = right_ref.shape[1] // 128

    def device(q, which):
        return (z, lax.div(q, 2), lax.rem(q, 2) * 2 + which)

    def other(i):
        return lax.rem(chip + i, 4)

    def on_line(i):
        return (lax.rem(z + i, 4), col, layer)

    partner = device(chip, 1 - core)
    above, below = (z + 1, col, layer), (z - 1, col, layer)
    has_above, has_below = z < 3, z > 0

    def remote(src, dst, send, recv, to):
        return pltpu.make_async_remote_copy(
            src_ref=src, dst_ref=dst, send_sem=send, recv_sem=recv, device_id=to, device_id_type=MESH)

    barrier = pltpu.get_barrier_semaphore()
    for to in [partner] + [on_line(i) for i in (1, 2, 3)] + [device(other(i), core) for i in (1, 2, 3)]:
        pl.semaphore_signal(barrier, inc=1, device_id=to, device_id_type=MESH)
    codes[z] = code_ref[...]

    def cut(k, carry):
        for m in range(strips):
            tiled[m * kblocks + k] = right_ref[pl.ds(pl.multiple_of(k * BLOCK, BLOCK), BLOCK), m * 128:(m + 1) * 128]
        return carry

    lax.fori_loop(0, kblocks, cut, 0)

    def pack(c):
        def one(t, carry):
            row, e = lax.div(t, 64), lax.rem(t, 64) * 2
            held[z, t] = join(
                tiled[pack_ref[row, e]], tiled[pack_ref[row, e + 1]],
                pack_ref[2 + row, e].astype(jnp.float32), pack_ref[4 + row, e].astype(jnp.float32),
                pack_ref[2 + row, e + 1].astype(jnp.float32), pack_ref[4 + row, e + 1].astype(jnp.float32))
            return carry
        lax.fori_loop(c * tiles, (c + 1) * tiles, one, 0)

    def up(j, c):
        piece = held.at[j, pl.ds(c * tiles, tiles)]
        return remote(piece, piece, zsend.at[0, j, c], zrecv.at[j, c], above)

    def down(j, c):
        piece = held.at[j, pl.ds(c * tiles, tiles)]
        return remote(piece, piece, zsend.at[1, j, c], zrecv.at[j, c], below)

    def tell(i):
        return remote(codes.at[z], codes.at[z], csend.at[i - 1], crecv.at[z], on_line(i))

    def told(i):
        j = lax.rem(z + i, 4)
        return remote(codes.at[j], codes.at[j], csend.at[i - 1], crecv.at[j], on_line(i))

    pack(0)
    pl.semaphore_wait(barrier, 7)
    for i in range(1, 4):
        tell(i).start()
    for c in range(CHUNKS):
        if c > 0:
            pack(c)

        @pl.when(has_above)
        def _():
            up(z, c).start()

        @pl.when(has_below)
        def _():
            down(z, c).start()

    depth = left_ref.shape[1]
    spread = (lax.broadcasted_iota(jnp.int32, (depth // BLOCK, depth), 1) // BLOCK
              == lax.broadcasted_iota(jnp.int32, (depth // BLOCK, depth), 0))
    lmask = jnp.dot(lpat_ref[...].astype(jnp.float32), jnp.where(spread, 1.0, 0.0),
                    preferred_element_type=jnp.float32)
    for i in range(rows // BLOCK):
        masked[i * BLOCK:(i + 1) * BLOCK, :] = (
            left_ref[i * BLOCK:(i + 1) * BLOCK, :] * lmask[i:i + 1, :].astype(jnp.bfloat16))

    for i in range(1, 4):
        told(i).wait_recv()
    to_scalars = pltpu.make_async_copy(codes, scalars, ssem)
    to_scalars.start()
    to_scalars.wait()
    flags[0] = jnp.maximum(jnp.maximum(codes[0], codes[1]), jnp.maximum(codes[2], codes[3]))
    pair = remote(flags.at[0], flags.at[1], gsend.at[0], grecv.at[0], partner)
    pair.start()

    def spread_flag(i):
        return remote(flags.at[2], flags.at[6 - i], gsend.at[i], grecv.at[4 - i], device(other(i), core))

    def flag_from(i):
        return remote(flags.at[2], flags.at[2 + i], gsend.at[i], grecv.at[i], device(other(i), core))

    def order(r):
        y = jnp.where(z < 2, z, 3 - z)
        o = jnp.where(r == 0, y, jnp.where(r == 1, y + 1, jnp.where(r == 2, 2 - 2 * y, 3)))
        return jnp.where(z < 2, o, 3 - o)

    def step(r, c):
        @pl.when((r > 0) & (z + r <= 3))
        def _():
            j = z + r
            down(j, c).wait_recv()

            @pl.when(has_below)
            def _():
                down(j, c).start()

        @pl.when((r > 0) & (z - r >= 0))
        def _():
            j = z - r
            up(j, c).wait_recv()

            @pl.when(has_above)
            def _():
                up(j, c).start()

    def expand(r, g):
        j = order(r)

        def fetch(t, carry):
            current[t] = held[j, t]
            return carry
        first = 0 if g == 0 else READY[g - 1]
        lax.fori_loop(first * tiles, READY[g] * tiles, fetch, 0)

        def one(k, carry):
            row, e = g // 2, (g % 2) * 64 + 2 * k
            wide[pl.ds(pl.multiple_of(k * BLOCK, BLOCK), BLOCK), :] = join(
                current[scalars[j, row, e]], current[scalars[j, row, e + 1]],
                scalars[j, 2 + row, e].astype(jnp.float32), scalars[j, 4 + row, e].astype(jnp.float32),
                scalars[j, 2 + row, e + 1].astype(jnp.float32), scalars[j, 4 + row, e + 1].astype(jnp.float32))
            return carry
        lax.fori_loop(0, kblocks, one, 0, unroll=4)

    def swap(n, q):
        return remote(part.at[n, q, 1 - core], swapped.at[n, q], xsend.at[n, q], xrecv.at[n, q], partner)

    def multiply(n):
        def one(i, carry):
            q = lax.rem(chip + 1 + i, 4)
            piece = jnp.dot(masked[pl.ds(pl.multiple_of(q * quarter, quarter), quarter), :], wide[...],
                            preferred_element_type=jnp.float32)
            part[n, q, 0] = piece[:eighth]
            part[n, q, 1] = piece[eighth:]
            swap(n, q).start()
            return carry
        lax.fori_loop(0, 4, one, 0)

    def scatter(n, i):
        return remote(part.at[n, other(i), core], got.at[n, 3 - i], rsend.at[n, i - 1], rrecv.at[n, 3 - i],
                      device(other(i), core))

    def arrival(n, i):
        return remote(part.at[n, chip, core], got.at[n, i - 1], rsend.at[n, i - 1], rrecv.at[n, i - 1],
                      device(other(i), core))

    def add_cores(n):
        for i in range(1, 5):
            q = other(i)
            swap(n, q).wait_recv()
            part[n, q, core] = part[n, q, core] + swapped[n, q]
            if i < 4:
                scatter(n, i).start()

    def deliver(n, to, which, place, source, source_core):
        rng = pl.ds(pl.multiple_of(source * quarter + source_core * eighth, eighth), eighth)
        return remote(done.at[n], out_ref.at[rng, pl.ds(pl.multiple_of(place * 128, 128), 128)],
                      fsend.at[n], frecv.at[place, source, source_core], device(to, which))

    def finish(n, r, g):
        j, which, place = order(r), g // 2, g % 2
        for i in range(1, 4):
            arrival(n, i).wait_recv()
        total = (part[n, chip, core] + got[n, 0]) + (got[n, 1] + got[n, 2])
        here = (j == chip) & (core == which)

        @pl.when(here)
        def _():
            rng = pl.ds(pl.multiple_of(chip * quarter + core * eighth, eighth), eighth)
            out_ref[rng, place * 128:(place + 1) * 128] = total.astype(jnp.bfloat16)

        @pl.when(jnp.logical_not(here))
        def _():
            done[n] = total.astype(jnp.bfloat16)
            deliver(n, j, which, place, chip, core).start()

    def rank(r, carry):
        for g in range(strips):
            n = r * strips + g
            for c in range(0 if g == 0 else READY[g - 1], READY[g]):
                step(r, c)
            expand(r, g)
            multiply(n)
            add_cores(n)
            if g > 0:
                finish(n - 1, r, g - 1)
            else:
                @pl.when(r > 0)
                def _():
                    finish(n - 1, r - 1, strips - 1)
        return carry

    pair.wait_recv()
    flags[2] = jnp.maximum(flags[0], flags[1])
    for i in range(1, 4):
        spread_flag(i).start()
    lax.fori_loop(0, 4, rank, 0)
    finish(4 * strips - 1, 3, strips - 1)

    for i in range(1, 4):
        flag_from(i).wait_recv()
    flag_ref[...] = jnp.maximum(jnp.maximum(flags[2], flags[3]), jnp.maximum(flags[4], flags[5]))
    pair.wait_send()
    for i in range(1, 4):
        spread_flag(i).wait_send()
        tell(i).wait_send()

    for place in range(2):
        for i in range(4):
            for source_core in range(2):
                @pl.when((i > 0) | (core != source_core))
                def _():
                    deliver(0, chip, core, place, other(i), source_core).wait_recv()

    def drain(r, carry):
        for g in range(strips):
            n = r * strips + g

            @pl.when((order(r) != chip) | (core != g // 2))
            def _():
                deliver(n, order(r), g // 2, g % 2, chip, core).wait_send()
            for q in range(4):
                swap(n, q).wait_send()
            for i in range(1, 4):
                scatter(n, i).wait_send()
        for c in range(CHUNKS):
            @pl.when(has_above & (r <= z))
            def _():
                up(r, c).wait_send()

            @pl.when(has_below & (r >= z))
            def _():
                down(r, c).wait_send()
        return carry

    lax.fori_loop(0, 4, drain, 0)


def run(left, lpat, right, code, pack):
    rows, width = left.shape[0], right.shape[1]
    eighth = rows // 8
    strips = width // 128
    units = 4 * strips
    dma = pltpu.SemaphoreType.DMA
    vmem = pl.BlockSpec(memory_space=pltpu.VMEM)
    smem = pl.BlockSpec(memory_space=pltpu.SMEM)
    tiles = (right.shape[0] // BLOCK) * strips
    return pl.pallas_call(
        kernel,
        out_shape=(jax.ShapeDtypeStruct((rows, width // 2), jnp.bfloat16),
                   jax.ShapeDtypeStruct((8, 128), jnp.int32)),
        in_specs=[vmem, vmem, vmem, vmem, smem],
        out_specs=(vmem, vmem),
        scratch_shapes=[
            pltpu.VMEM(left.shape, jnp.bfloat16),
            pltpu.VMEM((tiles, BLOCK, 128), jnp.bfloat16),
            pltpu.VMEM((4, CAP // 2, BLOCK, 128), jnp.bfloat16),
            pltpu.VMEM((CAP // 2, BLOCK, 128), jnp.bfloat16),
            pltpu.VMEM((right.shape[0], 128), jnp.bfloat16),
            pltpu.VMEM((units, 4, 2, eighth, 128), jnp.float32),
            pltpu.VMEM((units, 4, eighth, 128), jnp.float32),
            pltpu.VMEM((units, 3, eighth, 128), jnp.float32),
            pltpu.VMEM((units, eighth, 128), jnp.bfloat16),
            pltpu.VMEM((4, 8, 128), jnp.int32),
            pltpu.SMEM((4, 8, 128), jnp.int32),
            pltpu.VMEM((6, 8, 128), jnp.int32),
            dma((2, 4, CHUNKS)), dma((4, CHUNKS)),
            dma((units, 4)), dma((units, 4)), dma((units, 3)), dma((units, 3)),
            dma((units,)), dma((2, 4, 2)), dma((3,)), dma((4,)), dma, dma((4,)), dma((4,)),
        ],
        compiler_params=pltpu.CompilerParams(
            collective_id=0, has_side_effects=True, vmem_limit_bytes=56 * 2**20),
        name="sparse_product",
    )(left, lpat, right, code, pack)


def local_packed(left, lpat, right, rpat):
    kblocks, cols = rpat.shape
    present = rpat.reshape(kblocks, cols // 2, 2).transpose(1, 0, 2).reshape(-1)
    count = present.size
    upto = jnp.cumsum(present)
    slot = upto - present
    index = jnp.arange(count, dtype=jnp.int32)
    there = present > 0
    same = (slot - index) % 2 == 0
    ends = upto.reshape(cols // 2, -1)[:, -1]
    room = jnp.array([ready * (CAP // CHUNKS) for ready in READY], jnp.int32)
    over = jnp.any(ends > room).astype(jnp.int32)
    code = jnp.stack([
        jnp.where(there, jnp.minimum(slot // 2, CAP // 2 - 1), 0),
        (there & same).astype(jnp.int32),
        (there & jnp.logical_not(same)).astype(jnp.int32),
        jnp.broadcast_to(over, (count,)),
    ]).reshape(8, 128)
    hit = (slot[None, :] == index[:, None]) & there[None, :]
    source = jnp.sum(jnp.where(hit, index[None, :], 0), axis=1)
    keep = ((source - index) % 2 == 0).astype(jnp.int32)
    pack = jnp.stack([source // 2, keep, 1 - keep]).reshape(6, 128)
    out, flag = run(left, lpat, right, code, pack)
    return lax.cond(flag[6, 0] > 0, local_general, lambda *_: out, left, lpat, right, rpat)


def solution(mesh):
    placed = (
        P("row", ("layer", "col")),
        P("row", ("layer", "col")),
        P(("layer", "col"), "row"),
        P(("layer", "col"), "row"),
    )
    sizes = tuple(mesh.shape[axis] for axis in ("row", "col", "layer"))
    local = local_packed if sizes == (4, 2, 4) else local_general
    return jax.shard_map(
        local, mesh=mesh, in_specs=placed, out_specs=P("row", ("col", "layer")), check_vma=False
    )
```

```python
import functools

import jax
import jax.numpy as jnp
from jax import lax
from jax.experimental import pallas as pl
from jax.experimental.pallas import tpu as pltpu
from jax.sharding import PartitionSpec as P

MESH = pl.DeviceIdType.MESH
BLOCK = 64
CAP = 160
CHUNKS = 8
READY = (3, 5, 7, 8)


def from_behind(x, axis, by):
    size = lax.axis_size(axis)
    return lax.ppermute(x, axis, [(i, (i + by) % size) for i in range(size)])


def scatter_sum(partial_value):
    axes = ("col", "layer")
    size = lax.axis_size(axes)
    width = partial_value.shape[1] // size
    here = lax.axis_index("col") * lax.axis_size("layer") + lax.axis_index("layer")

    def share(owner):
        return lax.dynamic_slice_in_dim(partial_value, (owner % size) * width, width, 1)

    total = share(here)
    for away in range(1, size):
        total = total + from_behind(share(here + away), axes, away)
    return total


def apply_pattern(values, pattern):
    rows, cols = values.shape
    block = rows // pattern.shape[0]
    shaped = values.reshape(pattern.shape[0], block, pattern.shape[1], block)
    masked = shaped * pattern[:, None, :, None].astype(jnp.bfloat16)
    return masked.reshape(rows, cols)


def local_general(left_blocks, left_pattern, right_blocks, right_pattern):
    left = apply_pattern(left_blocks, left_pattern)
    right = apply_pattern(right_blocks, right_pattern)
    left_rows = left.shape[0]
    range_cols = right.shape[1]
    cycle_size = lax.axis_size("row")
    position = lax.axis_index("row")
    partial_value = jnp.zeros((left_rows, range_cols * cycle_size), jnp.float32)
    current = right
    for step in range(cycle_size):
        if step > 0:
            current = from_behind(current, "row", 1)
        owner = (position - step) % cycle_size
        piece = jnp.dot(left, current, preferred_element_type=jnp.float32)
        partial_value = lax.dynamic_update_slice_in_dim(partial_value, piece, owner * range_cols, 1)
    return scatter_sum(partial_value).astype(jnp.bfloat16)


def turn(tile):
    return jnp.concatenate([tile[:, BLOCK:], tile[:, :BLOCK]], axis=1)


def join(a, b, stay_a, turn_a, stay_b, turn_b):
    left = jnp.where(lax.broadcasted_iota(jnp.int32, (1, 128), 1) < BLOCK, 1.0, 0.0)
    right = 1.0 - left
    first = a * (left * stay_a).astype(jnp.bfloat16) + turn(a) * (left * turn_a).astype(jnp.bfloat16)
    second = b * (right * stay_b).astype(jnp.bfloat16) + turn(b) * (right * turn_b).astype(jnp.bfloat16)
    return first + second


def kernel(left_ref, lpat_ref, right_ref, code_ref, pack_ref, out_ref, flag_ref,
           masked, tiled, held, current, wide, part, swapped, got, done, codes, scalars, flags, flag_scalars,
           zsend, zrecv, xsend, xrecv, rsend, rrecv, fsend, frecv, csend, crecv, ssem, gsend, grecv):
    z = lax.axis_index("row")
    col = lax.axis_index("col")
    layer = lax.axis_index("layer")
    core = lax.rem(layer, 2)
    chip = col * 2 + lax.div(layer, 2)
    tiles = CAP // 2 // CHUNKS
    rows = left_ref.shape[0]
    quarter, eighth = rows // 4, rows // 8
    kblocks = right_ref.shape[0] // BLOCK
    strips = right_ref.shape[1] // 128

    def device(q, which):
        return (z, lax.div(q, 2), lax.rem(q, 2) * 2 + which)

    def other(i):
        return lax.rem(chip + i, 4)

    def on_line(i):
        return (lax.rem(z + i, 4), col, layer)

    partner = device(chip, 1 - core)
    above, below = (z + 1, col, layer), (z - 1, col, layer)
    has_above, has_below = z < 3, z > 0

    def remote(src, dst, send, recv, to):
        return pltpu.make_async_remote_copy(
            src_ref=src, dst_ref=dst, send_sem=send, recv_sem=recv, device_id=to, device_id_type=MESH)

    barrier = pltpu.get_barrier_semaphore()
    for to in [partner] + [on_line(i) for i in (1, 2, 3)] + [device(other(i), core) for i in (1, 2, 3)]:
        pl.semaphore_signal(barrier, inc=1, device_id=to, device_id_type=MESH)
    codes[z] = code_ref[...]

    def cut(k, carry):
        for m in range(strips):
            tiled[m * kblocks + k] = right_ref[pl.ds(pl.multiple_of(k * BLOCK, BLOCK), BLOCK), m * 128:(m + 1) * 128]
        return carry

    lax.fori_loop(0, kblocks, cut, 0)

    def pack(c):
        def one(t, carry):
            row, e = lax.div(t, 64), lax.rem(t, 64) * 2
            held[z, t] = join(
                tiled[pack_ref[row, e]], tiled[pack_ref[row, e + 1]],
                pack_ref[2 + row, e].astype(jnp.float32), pack_ref[4 + row, e].astype(jnp.float32),
                pack_ref[2 + row, e + 1].astype(jnp.float32), pack_ref[4 + row, e + 1].astype(jnp.float32))
            return carry
        lax.fori_loop(c * tiles, (c + 1) * tiles, one, 0)

    def up(j, c):
        piece = held.at[j, pl.ds(c * tiles, tiles)]
        return remote(piece, piece, zsend.at[0, j, c], zrecv.at[j, c], above)

    def down(j, c):
        piece = held.at[j, pl.ds(c * tiles, tiles)]
        return remote(piece, piece, zsend.at[1, j, c], zrecv.at[j, c], below)

    def tell(i):
        return remote(codes.at[z], codes.at[z], csend.at[i - 1], crecv.at[z], on_line(i))

    def told(i):
        j = lax.rem(z + i, 4)
        return remote(codes.at[j], codes.at[j], csend.at[i - 1], crecv.at[j], on_line(i))

    pack(0)
    pl.semaphore_wait(barrier, 7)
    for i in range(1, 4):
        tell(i).start()
    for c in range(CHUNKS):
        if c > 0:
            pack(c)

        @pl.when(has_above)
        def _():
            up(z, c).start()

        @pl.when(has_below)
        def _():
            down(z, c).start()

    depth = left_ref.shape[1]
    spread = (lax.broadcasted_iota(jnp.int32, (depth // BLOCK, depth), 1) // BLOCK
              == lax.broadcasted_iota(jnp.int32, (depth // BLOCK, depth), 0))
    lmask = jnp.dot(lpat_ref[...].astype(jnp.float32), jnp.where(spread, 1.0, 0.0),
                    preferred_element_type=jnp.float32)
    for i in range(rows // BLOCK):
        masked[i * BLOCK:(i + 1) * BLOCK, :] = (
            left_ref[i * BLOCK:(i + 1) * BLOCK, :] * lmask[i:i + 1, :].astype(jnp.bfloat16))

    for i in range(1, 4):
        told(i).wait_recv()
    to_scalars = pltpu.make_async_copy(codes, scalars, ssem)
    to_scalars.start()
    to_scalars.wait()
    flags[0] = jnp.maximum(jnp.maximum(codes[0], codes[1]), jnp.maximum(codes[2], codes[3]))
    pair = remote(flags.at[0], flags.at[1], gsend.at[0], grecv.at[0], partner)
    pair.start()

    def spread_flag(i):
        return remote(flags.at[2], flags.at[6 - i], gsend.at[i], grecv.at[4 - i], device(other(i), core))

    def flag_from(i):
        return remote(flags.at[2], flags.at[2 + i], gsend.at[i], grecv.at[i], device(other(i), core))

    def order(r):
        y = jnp.where(z < 2, z, 3 - z)
        o = jnp.where(r == 0, y, jnp.where(r == 1, y + 1, jnp.where(r == 2, 2 - 2 * y, 3)))
        return jnp.where(z < 2, o, 3 - o)

    def step(r, c):
        @pl.when((r > 0) & (z + r <= 3))
        def _():
            j = z + r
            down(j, c).wait_recv()

            @pl.when(has_below)
            def _():
                down(j, c).start()

        @pl.when((r > 0) & (z - r >= 0))
        def _():
            j = z - r
            up(j, c).wait_recv()

            @pl.when(has_above)
            def _():
                up(j, c).start()

    def expand(r, g):
        j = order(r)

        def fetch(t, carry):
            current[t] = held[j, t]
            return carry
        first = 0 if g == 0 else READY[g - 1]
        lax.fori_loop(first * tiles, READY[g] * tiles, fetch, 0)

        def one(k, carry):
            row, e = g // 2, (g % 2) * 64 + 2 * k
            wide[pl.ds(pl.multiple_of(k * BLOCK, BLOCK), BLOCK), :] = join(
                current[scalars[j, row, e]], current[scalars[j, row, e + 1]],
                scalars[j, 2 + row, e].astype(jnp.float32), scalars[j, 4 + row, e].astype(jnp.float32),
                scalars[j, 2 + row, e + 1].astype(jnp.float32), scalars[j, 4 + row, e + 1].astype(jnp.float32))
            return carry
        lax.fori_loop(0, kblocks, one, 0, unroll=4)

    def swap(n, q):
        return remote(part.at[n, q, 1 - core], swapped.at[n, q], xsend.at[n, q], xrecv.at[n, q], partner)

    def multiply(n):
        def one(i, carry):
            q = lax.rem(chip + 1 + i, 4)
            piece = jnp.dot(masked[pl.ds(pl.multiple_of(q * quarter, quarter), quarter), :], wide[...],
                            preferred_element_type=jnp.float32)
            part[n, q, 0] = piece[:eighth]
            part[n, q, 1] = piece[eighth:]
            swap(n, q).start()
            return carry
        lax.fori_loop(0, 4, one, 0)

    def scatter(n, i):
        return remote(part.at[n, other(i), core], got.at[n, 3 - i], rsend.at[n, i - 1], rrecv.at[n, 3 - i],
                      device(other(i), core))

    def arrival(n, i):
        return remote(part.at[n, chip, core], got.at[n, i - 1], rsend.at[n, i - 1], rrecv.at[n, i - 1],
                      device(other(i), core))

    def add_cores(n):
        for i in range(1, 5):
            q = other(i)
            swap(n, q).wait_recv()
            part[n, q, core] = part[n, q, core] + swapped[n, q]
            if i < 4:
                scatter(n, i).start()

    def deliver(n, to, which, place, source, source_core):
        rng = pl.ds(pl.multiple_of(source * quarter + source_core * eighth, eighth), eighth)
        return remote(done.at[n], out_ref.at[rng, pl.ds(pl.multiple_of(place * 128, 128), 128)],
                      fsend.at[n], frecv.at[place, source, source_core], device(to, which))

    def finish(n, r, g):
        j, which, place = order(r), g // 2, g % 2
        for i in range(1, 4):
            arrival(n, i).wait_recv()
        total = (part[n, chip, core] + got[n, 0]) + (got[n, 1] + got[n, 2])
        here = (j == chip) & (core == which)

        @pl.when(here)
        def _():
            rng = pl.ds(pl.multiple_of(chip * quarter + core * eighth, eighth), eighth)
            out_ref[rng, place * 128:(place + 1) * 128] = total.astype(jnp.bfloat16)

        @pl.when(jnp.logical_not(here))
        def _():
            done[n] = total.astype(jnp.bfloat16)
            deliver(n, j, which, place, chip, core).start()

    def rank(r, carry):
        for g in range(strips):
            n = r * strips + g
            for c in range(0 if g == 0 else READY[g - 1], READY[g]):
                step(r, c)
            expand(r, g)
            multiply(n)
            add_cores(n)
            if g > 0:
                finish(n - 1, r, g - 1)
            else:
                @pl.when(r > 0)
                def _():
                    finish(n - 1, r - 1, strips - 1)
        return carry

    pair.wait_recv()
    flags[2] = jnp.maximum(flags[0], flags[1])
    for i in range(1, 4):
        spread_flag(i).start()
    lax.fori_loop(0, 4, rank, 0)
    finish(4 * strips - 1, 3, strips - 1)

    for i in range(1, 4):
        flag_from(i).wait_recv()
    flags[6] = jnp.maximum(jnp.maximum(flags[2], flags[3]), jnp.maximum(flags[4], flags[5]))
    to_flag = pltpu.make_async_copy(flags.at[6], flag_scalars, ssem)
    to_flag.start()
    to_flag.wait()
    flag_ref[0] = flag_scalars[6, 0]
    pair.wait_send()
    for i in range(1, 4):
        spread_flag(i).wait_send()
        tell(i).wait_send()

    for place in range(2):
        for i in range(4):
            for source_core in range(2):
                @pl.when((i > 0) | (core != source_core))
                def _():
                    deliver(0, chip, core, place, other(i), source_core).wait_recv()

    def drain(r, carry):
        for g in range(strips):
            n = r * strips + g

            @pl.when((order(r) != chip) | (core != g // 2))
            def _():
                deliver(n, order(r), g // 2, g % 2, chip, core).wait_send()
            for q in range(4):
                swap(n, q).wait_send()
            for i in range(1, 4):
                scatter(n, i).wait_send()
        for c in range(CHUNKS):
            @pl.when(has_above & (r <= z))
            def _():
                up(r, c).wait_send()

            @pl.when(has_below & (r >= z))
            def _():
                down(r, c).wait_send()
        return carry

    lax.fori_loop(0, 4, drain, 0)


def run(left, lpat, right, code, pack):
    rows, width = left.shape[0], right.shape[1]
    eighth = rows // 8
    strips = width // 128
    units = 4 * strips
    dma = pltpu.SemaphoreType.DMA
    vmem = pl.BlockSpec(memory_space=pltpu.VMEM)
    smem = pl.BlockSpec(memory_space=pltpu.SMEM)
    tiles = (right.shape[0] // BLOCK) * strips
    return pl.pallas_call(
        kernel,
        out_shape=(jax.ShapeDtypeStruct((rows, width // 2), jnp.bfloat16),
                   jax.ShapeDtypeStruct((1,), jnp.int32)),
        in_specs=[vmem, vmem, vmem, vmem, smem],
        out_specs=(vmem, smem),
        scratch_shapes=[
            pltpu.VMEM(left.shape, jnp.bfloat16),
            pltpu.VMEM((tiles, BLOCK, 128), jnp.bfloat16),
            pltpu.VMEM((4, CAP // 2, BLOCK, 128), jnp.bfloat16),
            pltpu.VMEM((CAP // 2, BLOCK, 128), jnp.bfloat16),
            pltpu.VMEM((right.shape[0], 128), jnp.bfloat16),
            pltpu.VMEM((units, 4, 2, eighth, 128), jnp.float32),
            pltpu.VMEM((units, 4, eighth, 128), jnp.float32),
            pltpu.VMEM((units, 3, eighth, 128), jnp.float32),
            pltpu.VMEM((units, eighth, 128), jnp.bfloat16),
            pltpu.VMEM((4, 8, 128), jnp.int32),
            pltpu.SMEM((4, 8, 128), jnp.int32),
            pltpu.VMEM((7, 8, 128), jnp.int32),
            pltpu.SMEM((8, 128), jnp.int32),
            dma((2, 4, CHUNKS)), dma((4, CHUNKS)),
            dma((units, 4)), dma((units, 4)), dma((units, 3)), dma((units, 3)),
            dma((units,)), dma((2, 4, 2)), dma((3,)), dma((4,)), dma, dma((4,)), dma((4,)),
        ],
        compiler_params=pltpu.CompilerParams(
            collective_id=0, has_side_effects=True, vmem_limit_bytes=56 * 2**20),
        name="sparse_product",
    )(left, lpat, right, code, pack)


def local_packed(left, lpat, right, rpat):
    kblocks, cols = rpat.shape
    present = rpat.reshape(kblocks, cols // 2, 2).transpose(1, 0, 2).reshape(-1)
    count = present.size
    upto = jnp.cumsum(present)
    slot = upto - present
    index = jnp.arange(count, dtype=jnp.int32)
    there = present > 0
    same = (slot - index) % 2 == 0
    ends = upto.reshape(cols // 2, -1)[:, -1]
    room = jnp.array([ready * (CAP // CHUNKS) for ready in READY], jnp.int32)
    over = jnp.any(ends > room).astype(jnp.int32)
    code = jnp.stack([
        jnp.where(there, jnp.minimum(slot // 2, CAP // 2 - 1), 0),
        (there & same).astype(jnp.int32),
        (there & jnp.logical_not(same)).astype(jnp.int32),
        jnp.broadcast_to(over, (count,)),
    ]).reshape(8, 128)
    hit = (slot[None, :] == index[:, None]) & there[None, :]
    source = jnp.sum(jnp.where(hit, index[None, :], 0), axis=1)
    keep = ((source - index) % 2 == 0).astype(jnp.int32)
    pack = jnp.stack([source // 2, keep, 1 - keep]).reshape(6, 128)
    out, flag = run(left, lpat, right, code, pack)
    return lax.cond(flag[0] > 0, local_general, lambda *_: out, left, lpat, right, rpat)


def solution(mesh):
    placed = (
        P("row", ("layer", "col")),
        P("row", ("layer", "col")),
        P(("layer", "col"), "row"),
        P(("layer", "col"), "row"),
    )
    sizes = tuple(mesh.shape[axis] for axis in ("row", "col", "layer"))
    local = local_packed if sizes == (4, 2, 4) else local_general
    return jax.shard_map(
        local, mesh=mesh, in_specs=placed, out_specs=P("row", ("col", "layer")), check_vma=False
    )
```

```python
import functools

import jax
import jax.numpy as jnp
from jax import lax
from jax.experimental import pallas as pl
from jax.experimental.pallas import tpu as pltpu
from jax.sharding import PartitionSpec as P

MESH = pl.DeviceIdType.MESH
BLOCK = 64
CAP = 148
SPARE = 16
EDGES = (0, 10, 20, 30, 40, 50, 58, 66, 74)
CHUNKS = len(EDGES) - 1
READY = (3, 5, 7, 8)


def from_behind(x, axis, by):
    size = lax.axis_size(axis)
    return lax.ppermute(x, axis, [(i, (i + by) % size) for i in range(size)])


def scatter_sum(partial_value):
    axes = ("col", "layer")
    size = lax.axis_size(axes)
    width = partial_value.shape[1] // size
    here = lax.axis_index("col") * lax.axis_size("layer") + lax.axis_index("layer")

    def share(owner):
        return lax.dynamic_slice_in_dim(partial_value, (owner % size) * width, width, 1)

    total = share(here)
    for away in range(1, size):
        total = total + from_behind(share(here + away), axes, away)
    return total


def apply_pattern(values, pattern):
    rows, cols = values.shape
    block = rows // pattern.shape[0]
    shaped = values.reshape(pattern.shape[0], block, pattern.shape[1], block)
    masked = shaped * pattern[:, None, :, None].astype(jnp.bfloat16)
    return masked.reshape(rows, cols)


def local_general(left_blocks, left_pattern, right_blocks, right_pattern):
    left = apply_pattern(left_blocks, left_pattern)
    right = apply_pattern(right_blocks, right_pattern)
    left_rows = left.shape[0]
    range_cols = right.shape[1]
    cycle_size = lax.axis_size("row")
    position = lax.axis_index("row")
    partial_value = jnp.zeros((left_rows, range_cols * cycle_size), jnp.float32)
    current = right
    for step in range(cycle_size):
        if step > 0:
            current = from_behind(current, "row", 1)
        owner = (position - step) % cycle_size
        piece = jnp.dot(left, current, preferred_element_type=jnp.float32)
        partial_value = lax.dynamic_update_slice_in_dim(partial_value, piece, owner * range_cols, 1)
    return scatter_sum(partial_value).astype(jnp.bfloat16)


def turn(tile):
    return jnp.concatenate([tile[:, BLOCK:], tile[:, :BLOCK]], axis=1)


def join(a, b, stay_a, turn_a, stay_b, turn_b):
    left = jnp.where(lax.broadcasted_iota(jnp.int32, (1, 128), 1) < BLOCK, 1.0, 0.0)
    right = 1.0 - left
    first = a * (left * stay_a).astype(jnp.bfloat16) + turn(a) * (left * turn_a).astype(jnp.bfloat16)
    second = b * (right * stay_b).astype(jnp.bfloat16) + turn(b) * (right * turn_b).astype(jnp.bfloat16)
    return first + second


def prepare(pattern_ref, code_ref, pack_ref):
    kblocks, cols = pattern_ref.shape
    count = kblocks * cols
    per_strip = 2 * kblocks

    def iota(shape, axis):
        return lax.broadcasted_iota(jnp.int32, shape, axis)

    block = iota((cols, count), 1)
    choose = iota((cols, count), 0) == 2 * (block // per_strip) + block % 2
    spread = jnp.dot(pattern_ref[...].astype(jnp.float32), jnp.where(choose, 1.0, 0.0),
                     preferred_element_type=jnp.float32)
    mine = iota((kblocks, count), 0) == (iota((kblocks, count), 1) % per_strip) // 2
    present = jnp.sum(jnp.where(mine, spread, 0.0), axis=0, keepdims=True)
    before = jnp.where(iota((count, count), 0) < iota((count, count), 1), 1.0, 0.0)
    slot = jnp.dot(jnp.broadcast_to(present, (8, count)), before,
                   preferred_element_type=jnp.float32)[0:1].astype(jnp.int32)
    index = iota((1, count), 1)
    there = present > 0.5
    place = jnp.where(slot < CAP, slot, jnp.maximum(2 * CAP + SPARE - 1 - slot, CAP))
    same = place % 2 == index % 2

    eye = iota((count, count), 0) == iota((count, count), 1)
    column = jnp.sum(jnp.where(eye, jnp.where(there, place, -1).astype(jnp.float32), 0.0), axis=1, keepdims=True)
    hit = jnp.where(column.astype(jnp.int32) == iota((count, count), 1), 1.0, 0.0)
    source = jnp.sum(hit * iota((count, count), 0).astype(jnp.float32), axis=0, keepdims=True).astype(jnp.int32)
    used = jnp.sum(hit, axis=0, keepdims=True) > 0.5
    source = jnp.clip(source, 0, count - 1)
    level = source % 2 == index % 2

    total = jnp.sum(present, axis=1, keepdims=True)
    over = jnp.where(total > CAP + SPARE, 1.0, 0.0)
    for g in range(cols // 2 - 1):
        upto = jnp.sum(jnp.where(index < per_strip * (g + 1), present, 0.0), axis=1, keepdims=True)
        over = jnp.maximum(over, jnp.where(upto > 2 * EDGES[READY[g]], 1.0, 0.0))
    weight = jnp.broadcast_to(total + 4096.0 * over, (1, count)).astype(jnp.int32)

    def put(ref, row, value):
        ref[row:row + 1, :] = value[:, :128]
        ref[row + 1:row + 2, :] = value[:, 128:]

    put(code_ref, 0, jnp.where(there, place // 2, 0))
    put(code_ref, 2, jnp.where(there & same, 1, 0))
    put(code_ref, 4, jnp.where(there & jnp.logical_not(same), 1, 0))
    put(code_ref, 6, weight)
    put(pack_ref, 0, source // 2)
    put(pack_ref, 2, jnp.where(used & level, 1, 0))
    put(pack_ref, 4, jnp.where(used & jnp.logical_not(level), 1, 0))
    put(pack_ref, 6, jnp.zeros((1, count), jnp.int32))


def kernel(left_ref, lpat_ref, right_ref, code_ref, pack_ref, out_ref, flag_ref,
           masked, tiled, held, spill, foreign, lent, current, wide, part, swapped, got, done,
           codes, other_codes, scalars, flags, flag_scalars,
           zsend, zrecv, xsend, xrecv, rsend, rrecv, fsend, frecv, csend, crecv, ssem, gsend, grecv,
           spill_send, spill_recv, lend_send, lend_recv):
    z = lax.axis_index("row")
    col = lax.axis_index("col")
    layer = lax.axis_index("layer")
    core = lax.rem(layer, 2)
    chip = col * 2 + lax.div(layer, 2)
    tiles, last = CAP // 2, CAP // 2 - SPARE // 2
    rows = left_ref.shape[0]
    quarter, eighth = rows // 4, rows // 8
    kblocks = right_ref.shape[0] // BLOCK
    strips = right_ref.shape[1] // 128

    def device(q, which):
        return (z, lax.div(q, 2), lax.rem(q, 2) * 2 + which)

    def other(i):
        return lax.rem(chip + i, 4)

    def on_line(i):
        return (lax.rem(z + i, 4), col, layer)

    partner = device(chip, 1 - core)
    above, below = (z + 1, col, layer), (z - 1, col, layer)
    has_above, has_below = z < 3, z > 0

    def remote(src, dst, send, recv, to):
        return pltpu.make_async_remote_copy(
            src_ref=src, dst_ref=dst, send_sem=send, recv_sem=recv, device_id=to, device_id_type=MESH)

    barrier = pltpu.get_barrier_semaphore()
    for to in [partner] + [on_line(i) for i in (1, 2, 3)] + [device(other(i), core) for i in (1, 2, 3)]:
        pl.semaphore_signal(barrier, inc=1, device_id=to, device_id_type=MESH)
    codes[z] = code_ref[...]

    def cut(k, carry):
        for m in range(strips):
            tiled[m * kblocks + k] = right_ref[pl.ds(pl.multiple_of(k * BLOCK, BLOCK), BLOCK), m * 128:(m + 1) * 128]
        return carry

    lax.fori_loop(0, kblocks, cut, 0)

    def packed(t):
        row, e = lax.div(t, 64), lax.rem(t, 64) * 2
        return join(
            tiled[pack_ref[row, e]], tiled[pack_ref[row, e + 1]],
            pack_ref[2 + row, e].astype(jnp.float32), pack_ref[4 + row, e].astype(jnp.float32),
            pack_ref[2 + row, e + 1].astype(jnp.float32), pack_ref[4 + row, e + 1].astype(jnp.float32))

    def pack(c):
        def one(t, carry):
            held[z, t] = packed(t)
            return carry

        def with_foreign(t, carry):
            held[z, t] = packed(t) + foreign[t - last]
            return carry
        lax.fori_loop(EDGES[c], EDGES[c + 1], one if c < CHUNKS - 1 else with_foreign, 0)

    def pack_spill(t, carry):
        spill[t] = packed(tiles + t)
        return carry

    def span(c):
        return pl.ds(EDGES[c], EDGES[c + 1] - EDGES[c])

    def lend(r):
        return remote(held.at[order(r), pl.ds(last, SPARE // 2)], lent.at[r], lend_send.at[r], lend_recv.at[r], partner)

    def up(j, c):
        piece = held.at[j, span(c)]
        return remote(piece, piece, zsend.at[0, j, c], zrecv.at[j, c], above)

    def down(j, c):
        piece = held.at[j, span(c)]
        return remote(piece, piece, zsend.at[1, j, c], zrecv.at[j, c], below)

    def tell(i):
        return remote(codes.at[z], codes.at[z], csend.at[i - 1], crecv.at[z], on_line(i))

    def told(i):
        j = lax.rem(z + i, 4)
        return remote(codes.at[j], codes.at[j], csend.at[i - 1], crecv.at[j], on_line(i))

    pack(0)
    pl.semaphore_wait(barrier, 7)
    for i in range(1, 4):
        tell(i).start()
    spilled = remote(spill, foreign, spill_send, spill_recv, partner)
    for c in range(CHUNKS):
        if c == CHUNKS - 1:
            spilled.wait_recv()
        if c > 0:
            pack(c)

        @pl.when(has_above)
        def _():
            up(z, c).start()

        @pl.when(has_below)
        def _():
            down(z, c).start()

        if c == 0:
            lax.fori_loop(0, SPARE // 2, pack_spill, 0)
            spilled.start()

    depth = left_ref.shape[1]
    spread = (lax.broadcasted_iota(jnp.int32, (depth // BLOCK, depth), 1) // BLOCK
              == lax.broadcasted_iota(jnp.int32, (depth // BLOCK, depth), 0))
    lmask = jnp.dot(lpat_ref[...].astype(jnp.float32), jnp.where(spread, 1.0, 0.0),
                    preferred_element_type=jnp.float32)
    for i in range(rows // BLOCK):
        masked[i * BLOCK:(i + 1) * BLOCK, :] = (
            left_ref[i * BLOCK:(i + 1) * BLOCK, :] * lmask[i:i + 1, :].astype(jnp.bfloat16))

    for i in range(1, 4):
        told(i).wait_recv()
    to_scalars = pltpu.make_async_copy(codes, scalars, ssem)
    to_scalars.start()
    to_scalars.wait()
    pair = remote(codes, other_codes, gsend.at[0], grecv.at[0], partner)
    pair.start()

    def spread_flag(i):
        return remote(flags.at[2], flags.at[6 - i], gsend.at[i], grecv.at[4 - i], device(other(i), core))

    def flag_from(i):
        return remote(flags.at[2], flags.at[2 + i], gsend.at[i], grecv.at[i], device(other(i), core))

    def order(r):
        y = jnp.where(z < 2, z, 3 - z)
        o = jnp.where(r == 0, y, jnp.where(r == 1, y + 1, jnp.where(r == 2, 2 - 2 * y, 3)))
        return jnp.where(z < 2, o, 3 - o)

    def step(r, c):
        @pl.when((r > 0) & (z + r <= 3))
        def _():
            j = z + r
            down(j, c).wait_recv()

            @pl.when(has_below)
            def _():
                down(j, c).start()

        @pl.when((r > 0) & (z - r >= 0))
        def _():
            j = z - r
            up(j, c).wait_recv()

            @pl.when(has_above)
            def _():
                up(j, c).start()

    def expand(r, g):
        j = order(r)

        def fetch(t, carry):
            current[t] = held[j, t]
            return carry
        first = 0 if g == 0 else READY[g - 1]
        if g == strips - 1:
            lend(r).start()
        lax.fori_loop(EDGES[first], EDGES[READY[g]], fetch, 0)
        if g == strips - 1:
            lend(r).wait_recv()
            for t in range(SPARE // 2):
                current[tiles + t] = lent[r, t]

        def one(k, carry):
            row, e = g // 2, (g % 2) * 64 + 2 * k
            wide[pl.ds(pl.multiple_of(k * BLOCK, BLOCK), BLOCK), :] = join(
                current[scalars[j, row, e]], current[scalars[j, row, e + 1]],
                scalars[j, 2 + row, e].astype(jnp.float32), scalars[j, 4 + row, e].astype(jnp.float32),
                scalars[j, 2 + row, e + 1].astype(jnp.float32), scalars[j, 4 + row, e + 1].astype(jnp.float32))
            return carry
        lax.fori_loop(0, kblocks, one, 0, unroll=4)

    def swap(n, q):
        return remote(part.at[n, q, 1 - core], swapped.at[n, q], xsend.at[n, q], xrecv.at[n, q], partner)

    def multiply(n):
        def one(i, carry):
            q = lax.rem(chip + 1 + i, 4)
            piece = jnp.dot(masked[pl.ds(pl.multiple_of(q * quarter, quarter), quarter), :], wide[...],
                            preferred_element_type=jnp.float32)
            part[n, q, 0] = piece[:eighth]
            part[n, q, 1] = piece[eighth:]
            swap(n, q).start()
            return carry
        lax.fori_loop(0, 4, one, 0)

    def scatter(n, i):
        return remote(part.at[n, other(i), core], got.at[n, 3 - i], rsend.at[n, i - 1], rrecv.at[n, 3 - i],
                      device(other(i), core))

    def arrival(n, i):
        return remote(part.at[n, chip, core], got.at[n, i - 1], rsend.at[n, i - 1], rrecv.at[n, i - 1],
                      device(other(i), core))

    def add_cores(n):
        for i in range(1, 5):
            q = other(i)
            swap(n, q).wait_recv()
            part[n, q, core] = part[n, q, core] + swapped[n, q]
            if i < 4:
                scatter(n, i).start()

    def deliver(n, to, which, place, source, source_core):
        rng = pl.ds(pl.multiple_of(source * quarter + source_core * eighth, eighth), eighth)
        return remote(done.at[n], out_ref.at[rng, pl.ds(pl.multiple_of(place * 128, 128), 128)],
                      fsend.at[n], frecv.at[place, source, source_core], device(to, which))

    def finish(n, r, g):
        j, which, place = order(r), g // 2, g % 2
        for i in range(1, 4):
            arrival(n, i).wait_recv()
        total = (part[n, chip, core] + got[n, 0]) + (got[n, 1] + got[n, 2])
        here = (j == chip) & (core == which)

        @pl.when(here)
        def _():
            rng = pl.ds(pl.multiple_of(chip * quarter + core * eighth, eighth), eighth)
            out_ref[rng, place * 128:(place + 1) * 128] = total.astype(jnp.bfloat16)

        @pl.when(jnp.logical_not(here))
        def _():
            done[n] = total.astype(jnp.bfloat16)
            deliver(n, j, which, place, chip, core).start()

    def rank(r, carry):
        for g in range(strips):
            n = r * strips + g
            for c in range(0 if g == 0 else READY[g - 1], READY[g]):
                step(r, c)
            expand(r, g)
            multiply(n)
            add_cores(n)
            if g > 0:
                finish(n - 1, r, g - 1)
            else:
                @pl.when(r > 0)
                def _():
                    finish(n - 1, r - 1, strips - 1)
        return carry

    pair.wait_recv()
    sums = [codes[j] + other_codes[j] for j in range(4)]
    flags[2] = jnp.maximum(jnp.maximum(sums[0], sums[1]), jnp.maximum(sums[2], sums[3]))
    for i in range(1, 4):
        spread_flag(i).start()
    lax.fori_loop(0, 4, rank, 0)
    finish(4 * strips - 1, 3, strips - 1)

    for i in range(1, 4):
        flag_from(i).wait_recv()
    flags[6] = jnp.maximum(jnp.maximum(flags[2], flags[3]), jnp.maximum(flags[4], flags[5]))
    to_flag = pltpu.make_async_copy(flags.at[6], flag_scalars, ssem)
    to_flag.start()
    to_flag.wait()
    flag_ref[0] = flag_scalars[6, 0]
    pair.wait_send()
    spilled.wait_send()
    for i in range(1, 4):
        spread_flag(i).wait_send()
        tell(i).wait_send()

    for place in range(2):
        for i in range(4):
            for source_core in range(2):
                @pl.when((i > 0) | (core != source_core))
                def _():
                    deliver(0, chip, core, place, other(i), source_core).wait_recv()

    def drain(r, carry):
        for g in range(strips):
            n = r * strips + g

            if g == 0:
                lend(r).wait_send()

            @pl.when((order(r) != chip) | (core != g // 2))
            def _():
                deliver(n, order(r), g // 2, g % 2, chip, core).wait_send()
            for q in range(4):
                swap(n, q).wait_send()
            for i in range(1, 4):
                scatter(n, i).wait_send()
        for c in range(CHUNKS):
            @pl.when(has_above & (r <= z))
            def _():
                up(r, c).wait_send()

            @pl.when(has_below & (r >= z))
            def _():
                down(r, c).wait_send()
        return carry

    lax.fori_loop(0, 4, drain, 0)


def run(left, lpat, right, code, pack):
    rows, width = left.shape[0], right.shape[1]
    eighth = rows // 8
    strips = width // 128
    units = 4 * strips
    dma = pltpu.SemaphoreType.DMA
    vmem = pl.BlockSpec(memory_space=pltpu.VMEM)
    smem = pl.BlockSpec(memory_space=pltpu.SMEM)
    tiles = (right.shape[0] // BLOCK) * strips
    return pl.pallas_call(
        kernel,
        out_shape=(jax.ShapeDtypeStruct((rows, width // 2), jnp.bfloat16),
                   jax.ShapeDtypeStruct((1,), jnp.int32)),
        in_specs=[vmem, vmem, vmem, vmem, smem],
        out_specs=(vmem, smem),
        scratch_shapes=[
            pltpu.VMEM(left.shape, jnp.bfloat16),
            pltpu.VMEM((tiles, BLOCK, 128), jnp.bfloat16),
            pltpu.VMEM((4, CAP // 2, BLOCK, 128), jnp.bfloat16),
            pltpu.VMEM((SPARE // 2, BLOCK, 128), jnp.bfloat16),
            pltpu.VMEM((SPARE // 2, BLOCK, 128), jnp.bfloat16),
            pltpu.VMEM((4, SPARE // 2, BLOCK, 128), jnp.bfloat16),
            pltpu.VMEM((CAP // 2 + SPARE // 2, BLOCK, 128), jnp.bfloat16),
            pltpu.VMEM((right.shape[0], 128), jnp.bfloat16),
            pltpu.VMEM((units, 4, 2, eighth, 128), jnp.float32),
            pltpu.VMEM((units, 4, eighth, 128), jnp.float32),
            pltpu.VMEM((units, 3, eighth, 128), jnp.float32),
            pltpu.VMEM((units, eighth, 128), jnp.bfloat16),
            pltpu.VMEM((4, 8, 128), jnp.int32),
            pltpu.VMEM((4, 8, 128), jnp.int32),
            pltpu.SMEM((4, 8, 128), jnp.int32),
            pltpu.VMEM((7, 8, 128), jnp.int32),
            pltpu.SMEM((8, 128), jnp.int32),
            dma((2, 4, CHUNKS)), dma((4, CHUNKS)),
            dma((units, 4)), dma((units, 4)), dma((units, 3)), dma((units, 3)),
            dma((units,)), dma((2, 4, 2)), dma((3,)), dma((4,)), dma, dma((4,)), dma((4,)),
            dma, dma, dma((4,)), dma((4,)),
        ],
        compiler_params=pltpu.CompilerParams(
            collective_id=0, has_side_effects=True, vmem_limit_bytes=56 * 2**20),
        name="sparse_product",
    )(left, lpat, right, code, pack)


def local_packed(left, lpat, right, rpat):
    table = jax.ShapeDtypeStruct((8, 128), jnp.int32)
    vmem = pl.BlockSpec(memory_space=pltpu.VMEM)
    code, pack = pl.pallas_call(
        prepare, out_shape=(table, table), in_specs=[vmem], out_specs=(vmem, vmem), name="places")(rpat)
    out, flag = run(left, lpat, right, code, pack)
    return lax.cond(flag[0] > 2 * CAP, local_general, lambda *_: out, left, lpat, right, rpat)


def solution(mesh):
    placed = (
        P("row", ("layer", "col")),
        P("row", ("layer", "col")),
        P(("layer", "col"), "row"),
        P(("layer", "col"), "row"),
    )
    sizes = tuple(mesh.shape[axis] for axis in ("row", "col", "layer"))
    local = local_packed if sizes == (4, 2, 4) else local_general
    return jax.shard_map(
        local, mesh=mesh, in_specs=placed, out_specs=P("row", ("col", "layer")), check_vma=False
    )
```

```python
import functools

import jax
import jax.numpy as jnp
from jax import lax
from jax.experimental import pallas as pl
from jax.experimental.pallas import tpu as pltpu
from jax.sharding import PartitionSpec as P

MESH = pl.DeviceIdType.MESH
BLOCK = 64
CAP = 148
SPARE = 16
EDGES = (0, 10, 20, 30, 40, 50, 58, 66, 74)
CHUNKS = len(EDGES) - 1
READY = (3, 5, 7, 8)


def from_behind(x, axis, by):
    size = lax.axis_size(axis)
    return lax.ppermute(x, axis, [(i, (i + by) % size) for i in range(size)])


def scatter_sum(partial_value):
    axes = ("col", "layer")
    size = lax.axis_size(axes)
    width = partial_value.shape[1] // size
    here = lax.axis_index("col") * lax.axis_size("layer") + lax.axis_index("layer")

    def share(owner):
        return lax.dynamic_slice_in_dim(partial_value, (owner % size) * width, width, 1)

    total = share(here)
    for away in range(1, size):
        total = total + from_behind(share(here + away), axes, away)
    return total


def apply_pattern(values, pattern):
    rows, cols = values.shape
    block = rows // pattern.shape[0]
    shaped = values.reshape(pattern.shape[0], block, pattern.shape[1], block)
    masked = shaped * pattern[:, None, :, None].astype(jnp.bfloat16)
    return masked.reshape(rows, cols)


def local_general(left_blocks, left_pattern, right_blocks, right_pattern):
    left = apply_pattern(left_blocks, left_pattern)
    right = apply_pattern(right_blocks, right_pattern)
    left_rows = left.shape[0]
    range_cols = right.shape[1]
    cycle_size = lax.axis_size("row")
    position = lax.axis_index("row")
    partial_value = jnp.zeros((left_rows, range_cols * cycle_size), jnp.float32)
    current = right
    for step in range(cycle_size):
        if step > 0:
            current = from_behind(current, "row", 1)
        owner = (position - step) % cycle_size
        piece = jnp.dot(left, current, preferred_element_type=jnp.float32)
        partial_value = lax.dynamic_update_slice_in_dim(partial_value, piece, owner * range_cols, 1)
    return scatter_sum(partial_value).astype(jnp.bfloat16)


def turn(tile):
    return jnp.concatenate([tile[:, BLOCK:], tile[:, :BLOCK]], axis=1)


def join(a, b):
    left = jnp.where(lax.broadcasted_iota(jnp.int32, (1, 128), 1) < BLOCK, 1.0, 0.0)
    return a * left.astype(jnp.bfloat16) + b * (1.0 - left).astype(jnp.bfloat16)


def prepare(pattern_ref, code_ref, pack_ref):
    kblocks, cols = pattern_ref.shape
    count = kblocks * cols
    per_strip = 2 * kblocks

    def iota(shape, axis):
        return lax.broadcasted_iota(jnp.int32, shape, axis)

    block = iota((cols, count), 1)
    choose = iota((cols, count), 0) == 2 * (block // per_strip) + block % 2
    spread = jnp.dot(pattern_ref[...].astype(jnp.float32), jnp.where(choose, 1.0, 0.0),
                     preferred_element_type=jnp.float32)
    mine = iota((kblocks, count), 0) == (iota((kblocks, count), 1) % per_strip) // 2
    present = jnp.sum(jnp.where(mine, spread, 0.0), axis=0, keepdims=True)
    before = jnp.where(iota((count, count), 0) < iota((count, count), 1), 1.0, 0.0)
    slot = jnp.dot(jnp.broadcast_to(present, (8, count)), before,
                   preferred_element_type=jnp.float32)[0:1].astype(jnp.int32)
    index = iota((1, count), 1)
    there = present > 0.5
    place = jnp.where(slot < CAP, slot, jnp.maximum(2 * CAP + SPARE - 1 - slot, CAP))
    same = place % 2 == index % 2

    eye = iota((count, count), 0) == iota((count, count), 1)
    column = jnp.sum(jnp.where(eye, jnp.where(there, place, -1).astype(jnp.float32), 0.0), axis=1, keepdims=True)
    hit = jnp.where(column.astype(jnp.int32) == iota((count, count), 1), 1.0, 0.0)
    source = jnp.sum(hit * iota((count, count), 0).astype(jnp.float32), axis=0, keepdims=True).astype(jnp.int32)
    used = jnp.sum(hit, axis=0, keepdims=True) > 0.5
    source = jnp.clip(source, 0, count - 1)
    level = source % 2 == index % 2

    total = jnp.sum(present, axis=1, keepdims=True)
    over = jnp.where(total > CAP + SPARE, 1.0, 0.0)
    for g in range(cols // 2 - 1):
        upto = jnp.sum(jnp.where(index < per_strip * (g + 1), present, 0.0), axis=1, keepdims=True)
        over = jnp.maximum(over, jnp.where(upto > 2 * EDGES[READY[g]], 1.0, 0.0))
    weight = jnp.broadcast_to(total + 4096.0 * over, (1, count)).astype(jnp.int32)

    def put(ref, row, value):
        ref[row:row + 1, :] = value[:, :128]
        ref[row + 1:row + 2, :] = value[:, 128:]

    tiles = (CAP + SPARE) // 2
    put(code_ref, 0, jnp.where(there, place // 2 + jnp.where(same, 0, tiles), 2 * tiles))
    put(code_ref, 2, weight)
    put(pack_ref, 0, jnp.where(used, source // 2 + jnp.where(level, 0, count // 2), count))
    for ref, row in ((code_ref, 4), (code_ref, 6), (pack_ref, 2), (pack_ref, 4), (pack_ref, 6)):
        put(ref, row, jnp.zeros((1, count), jnp.int32))


def kernel(left_ref, lpat_ref, right_ref, code_ref, pack_ref, out_ref, flag_ref,
           masked, tiled, held, spill, foreign, lent, current, wide, part, swapped, got, done,
           codes, other_codes, scalars, flags, flag_scalars,
           zsend, zrecv, xsend, xrecv, rsend, rrecv, fsend, frecv, csend, crecv, ssem, gsend, grecv,
           spill_send, spill_recv, lend_send, lend_recv):
    z = lax.axis_index("row")
    col = lax.axis_index("col")
    layer = lax.axis_index("layer")
    core = lax.rem(layer, 2)
    chip = col * 2 + lax.div(layer, 2)
    tiles, last, most = CAP // 2, CAP // 2 - SPARE // 2, CAP // 2 + SPARE // 2
    rows = left_ref.shape[0]
    quarter, eighth = rows // 4, rows // 8
    kblocks = right_ref.shape[0] // BLOCK
    strips = right_ref.shape[1] // 128

    def device(q, which):
        return (z, lax.div(q, 2), lax.rem(q, 2) * 2 + which)

    def other(i):
        return lax.rem(chip + i, 4)

    def on_line(i):
        return (lax.rem(z + i, 4), col, layer)

    partner = device(chip, 1 - core)
    above, below = (z + 1, col, layer), (z - 1, col, layer)
    has_above, has_below = z < 3, z > 0

    def remote(src, dst, send, recv, to):
        return pltpu.make_async_remote_copy(
            src_ref=src, dst_ref=dst, send_sem=send, recv_sem=recv, device_id=to, device_id_type=MESH)

    barrier = pltpu.get_barrier_semaphore()
    for to in [partner] + [on_line(i) for i in (1, 2, 3)] + [device(other(i), core) for i in (1, 2, 3)]:
        pl.semaphore_signal(barrier, inc=1, device_id=to, device_id_type=MESH)
    codes[z] = code_ref[...]

    def cut(k, carry):
        for m in range(strips):
            tile = right_ref[pl.ds(pl.multiple_of(k * BLOCK, BLOCK), BLOCK), m * 128:(m + 1) * 128]
            tiled[m * kblocks + k] = tile
            tiled[(strips + m) * kblocks + k] = turn(tile)
        return carry

    lax.fori_loop(0, kblocks, cut, 0, unroll=2)
    tiled[2 * strips * kblocks] = jnp.zeros((BLOCK, 128), jnp.bfloat16)
    current[2 * most] = jnp.zeros((BLOCK, 128), jnp.bfloat16)

    def packed(t):
        row, e = lax.div(t, 64), lax.rem(t, 64) * 2
        return join(tiled[pack_ref[row, e]], tiled[pack_ref[row, e + 1]])

    def pack(c):
        def one(t, carry):
            held[z, t] = packed(t)
            return carry

        def with_foreign(t, carry):
            held[z, t] = packed(t) + foreign[t - last]
            return carry
        lax.fori_loop(EDGES[c], EDGES[c + 1], one if c < CHUNKS - 1 else with_foreign, 0)

    def pack_spill(t, carry):
        spill[t] = packed(tiles + t)
        return carry

    def span(c):
        return pl.ds(EDGES[c], EDGES[c + 1] - EDGES[c])

    def lend(r):
        return remote(held.at[order(r), pl.ds(last, SPARE // 2)], lent.at[r], lend_send.at[r], lend_recv.at[r], partner)

    def up(j, c):
        piece = held.at[j, span(c)]
        return remote(piece, piece, zsend.at[0, j, c], zrecv.at[j, c], above)

    def down(j, c):
        piece = held.at[j, span(c)]
        return remote(piece, piece, zsend.at[1, j, c], zrecv.at[j, c], below)

    def tell(i):
        return remote(codes.at[z], codes.at[z], csend.at[i - 1], crecv.at[z], on_line(i))

    def told(i):
        j = lax.rem(z + i, 4)
        return remote(codes.at[j], codes.at[j], csend.at[i - 1], crecv.at[j], on_line(i))

    pack(0)
    pl.semaphore_wait(barrier, 7)
    for i in range(1, 4):
        tell(i).start()
    spilled = remote(spill, foreign, spill_send, spill_recv, partner)
    for c in range(CHUNKS):
        if c == CHUNKS - 1:
            spilled.wait_recv()
        if c > 0:
            pack(c)

        @pl.when(has_above)
        def _():
            up(z, c).start()

        @pl.when(has_below)
        def _():
            down(z, c).start()

        if c == 0:
            lax.fori_loop(0, SPARE // 2, pack_spill, 0)
            spilled.start()

    depth = left_ref.shape[1]
    spread = (lax.broadcasted_iota(jnp.int32, (depth // BLOCK, depth), 1) // BLOCK
              == lax.broadcasted_iota(jnp.int32, (depth // BLOCK, depth), 0))
    lmask = jnp.dot(lpat_ref[...].astype(jnp.float32), jnp.where(spread, 1.0, 0.0),
                    preferred_element_type=jnp.float32)
    for i in range(rows // BLOCK):
        masked[i * BLOCK:(i + 1) * BLOCK, :] = (
            left_ref[i * BLOCK:(i + 1) * BLOCK, :] * lmask[i:i + 1, :].astype(jnp.bfloat16))

    for i in range(1, 4):
        told(i).wait_recv()
    to_scalars = pltpu.make_async_copy(codes, scalars, ssem)
    to_scalars.start()
    to_scalars.wait()
    pair = remote(codes, other_codes, gsend.at[0], grecv.at[0], partner)
    pair.start()

    def spread_flag(i):
        return remote(flags.at[2], flags.at[6 - i], gsend.at[i], grecv.at[4 - i], device(other(i), core))

    def flag_from(i):
        return remote(flags.at[2], flags.at[2 + i], gsend.at[i], grecv.at[i], device(other(i), core))

    def order(r):
        y = jnp.where(z < 2, z, 3 - z)
        o = jnp.where(r == 0, y, jnp.where(r == 1, y + 1, jnp.where(r == 2, 2 - 2 * y, 3)))
        return jnp.where(z < 2, o, 3 - o)

    def step(r, c):
        @pl.when((r > 0) & (z + r <= 3))
        def _():
            j = z + r
            down(j, c).wait_recv()

            @pl.when(has_below)
            def _():
                down(j, c).start()

        @pl.when((r > 0) & (z - r >= 0))
        def _():
            j = z - r
            up(j, c).wait_recv()

            @pl.when(has_above)
            def _():
                up(j, c).start()

    def expand(r, g):
        j = order(r)

        def fetch(t, carry):
            current[t] = held[j, t]
            current[most + t] = turn(held[j, t])
            return carry
        first = 0 if g == 0 else READY[g - 1]
        if g == strips - 1:
            lend(r).start()
        lax.fori_loop(EDGES[first], EDGES[READY[g]], fetch, 0, unroll=2)
        if g == strips - 1:
            lend(r).wait_recv()
            for t in range(SPARE // 2):
                current[tiles + t] = lent[r, t]
                current[most + tiles + t] = turn(lent[r, t])

        def one(k, carry):
            row, e = g // 2, (g % 2) * 64 + 2 * k
            wide[pl.ds(pl.multiple_of(k * BLOCK, BLOCK), BLOCK), :] = join(
                current[scalars[j, row, e]], current[scalars[j, row, e + 1]])
            return carry
        lax.fori_loop(0, kblocks, one, 0, unroll=4)

    def swap(n, q):
        return remote(part.at[n, q, 1 - core], swapped.at[n, q], xsend.at[n, q], xrecv.at[n, q], partner)

    def multiply(n):
        def one(i, carry):
            pair = lax.rem(lax.div(chip, 2) + 1 + i, 2)
            piece = jnp.dot(masked[pl.ds(pl.multiple_of(pair * 2 * quarter, quarter), 2 * quarter), :], wide[...],
                            preferred_element_type=jnp.float32)
            for k in range(2):
                q = pair * 2 + k
                part[n, q, 0] = piece[2 * k * eighth:(2 * k + 1) * eighth]
                part[n, q, 1] = piece[(2 * k + 1) * eighth:(2 * k + 2) * eighth]
                swap(n, q).start()
            return carry
        lax.fori_loop(0, 2, one, 0)

    def scatter(n, i):
        return remote(part.at[n, other(i), core], got.at[n, 3 - i], rsend.at[n, i - 1], rrecv.at[n, 3 - i],
                      device(other(i), core))

    def arrival(n, i):
        return remote(part.at[n, chip, core], got.at[n, i - 1], rsend.at[n, i - 1], rrecv.at[n, i - 1],
                      device(other(i), core))

    def add_cores(n):
        for i in range(1, 5):
            q = other(i)
            swap(n, q).wait_recv()
            part[n, q, core] = part[n, q, core] + swapped[n, q]
            if i < 4:
                scatter(n, i).start()

    def deliver(n, to, which, place, source, source_core):
        rng = pl.ds(pl.multiple_of(source * quarter + source_core * eighth, eighth), eighth)
        return remote(done.at[n], out_ref.at[rng, pl.ds(pl.multiple_of(place * 128, 128), 128)],
                      fsend.at[n], frecv.at[place, source, source_core], device(to, which))

    def finish(n, r, g):
        j, which, place = order(r), g // 2, g % 2
        for i in range(1, 4):
            arrival(n, i).wait_recv()
        total = (part[n, chip, core] + got[n, 0]) + (got[n, 1] + got[n, 2])
        here = (j == chip) & (core == which)

        @pl.when(here)
        def _():
            rng = pl.ds(pl.multiple_of(chip * quarter + core * eighth, eighth), eighth)
            out_ref[rng, place * 128:(place + 1) * 128] = total.astype(jnp.bfloat16)

        @pl.when(jnp.logical_not(here))
        def _():
            done[n] = total.astype(jnp.bfloat16)
            deliver(n, j, which, place, chip, core).start()

    def rank(r, carry):
        for g in range(strips):
            n = r * strips + g
            for c in range(0 if g == 0 else READY[g - 1], READY[g]):
                step(r, c)
            expand(r, g)
            multiply(n)
            add_cores(n)
            if g > 0:
                finish(n - 1, r, g - 1)
            else:
                @pl.when(r > 0)
                def _():
                    finish(n - 1, r - 1, strips - 1)
        return carry

    pair.wait_recv()
    sums = [codes[j] + other_codes[j] for j in range(4)]
    flags[2] = jnp.maximum(jnp.maximum(sums[0], sums[1]), jnp.maximum(sums[2], sums[3]))
    for i in range(1, 4):
        spread_flag(i).start()
    lax.fori_loop(0, 4, rank, 0)
    finish(4 * strips - 1, 3, strips - 1)

    for i in range(1, 4):
        flag_from(i).wait_recv()
    flags[6] = jnp.maximum(jnp.maximum(flags[2], flags[3]), jnp.maximum(flags[4], flags[5]))
    to_flag = pltpu.make_async_copy(flags.at[6], flag_scalars, ssem)
    to_flag.start()
    to_flag.wait()
    flag_ref[0] = flag_scalars[2, 0]
    pair.wait_send()
    spilled.wait_send()
    for i in range(1, 4):
        spread_flag(i).wait_send()
        tell(i).wait_send()

    for place in range(2):
        for i in range(4):
            for source_core in range(2):
                @pl.when((i > 0) | (core != source_core))
                def _():
                    deliver(0, chip, core, place, other(i), source_core).wait_recv()

    def drain(r, carry):
        for g in range(strips):
            n = r * strips + g

            if g == 0:
                lend(r).wait_send()

            @pl.when((order(r) != chip) | (core != g // 2))
            def _():
                deliver(n, order(r), g // 2, g % 2, chip, core).wait_send()
            for q in range(4):
                swap(n, q).wait_send()
            for i in range(1, 4):
                scatter(n, i).wait_send()
        for c in range(CHUNKS):
            @pl.when(has_above & (r <= z))
            def _():
                up(r, c).wait_send()

            @pl.when(has_below & (r >= z))
            def _():
                down(r, c).wait_send()
        return carry

    lax.fori_loop(0, 4, drain, 0)


def run(left, lpat, right, code, pack):
    rows, width = left.shape[0], right.shape[1]
    eighth = rows // 8
    strips = width // 128
    units = 4 * strips
    dma = pltpu.SemaphoreType.DMA
    vmem = pl.BlockSpec(memory_space=pltpu.VMEM)
    smem = pl.BlockSpec(memory_space=pltpu.SMEM)
    tiles = (right.shape[0] // BLOCK) * strips
    return pl.pallas_call(
        kernel,
        out_shape=(jax.ShapeDtypeStruct((rows, width // 2), jnp.bfloat16),
                   jax.ShapeDtypeStruct((1,), jnp.int32)),
        in_specs=[vmem, vmem, vmem, vmem, smem],
        out_specs=(vmem, smem),
        scratch_shapes=[
            pltpu.VMEM(left.shape, jnp.bfloat16),
            pltpu.VMEM((2 * tiles + 1, BLOCK, 128), jnp.bfloat16),
            pltpu.VMEM((4, CAP // 2, BLOCK, 128), jnp.bfloat16),
            pltpu.VMEM((SPARE // 2, BLOCK, 128), jnp.bfloat16),
            pltpu.VMEM((SPARE // 2, BLOCK, 128), jnp.bfloat16),
            pltpu.VMEM((4, SPARE // 2, BLOCK, 128), jnp.bfloat16),
            pltpu.VMEM((CAP + SPARE + 1, BLOCK, 128), jnp.bfloat16),
            pltpu.VMEM((right.shape[0], 128), jnp.bfloat16),
            pltpu.VMEM((units, 4, 2, eighth, 128), jnp.float32),
            pltpu.VMEM((units, 4, eighth, 128), jnp.float32),
            pltpu.VMEM((units, 3, eighth, 128), jnp.float32),
            pltpu.VMEM((units, eighth, 128), jnp.bfloat16),
            pltpu.VMEM((4, 8, 128), jnp.int32),
            pltpu.VMEM((4, 8, 128), jnp.int32),
            pltpu.SMEM((4, 8, 128), jnp.int32),
            pltpu.VMEM((7, 8, 128), jnp.int32),
            pltpu.SMEM((8, 128), jnp.int32),
            dma((2, 4, CHUNKS)), dma((4, CHUNKS)),
            dma((units, 4)), dma((units, 4)), dma((units, 3)), dma((units, 3)),
            dma((units,)), dma((2, 4, 2)), dma((3,)), dma((4,)), dma, dma((4,)), dma((4,)),
            dma, dma, dma((4,)), dma((4,)),
        ],
        compiler_params=pltpu.CompilerParams(
            collective_id=0, has_side_effects=True, vmem_limit_bytes=56 * 2**20),
        name="sparse_product",
    )(left, lpat, right, code, pack)


def local_packed(left, lpat, right, rpat):
    table = jax.ShapeDtypeStruct((8, 128), jnp.int32)
    vmem = pl.BlockSpec(memory_space=pltpu.VMEM)
    code, pack = pl.pallas_call(
        prepare, out_shape=(table, table), in_specs=[vmem], out_specs=(vmem, vmem), name="places")(rpat)
    out, flag = run(left, lpat, right, code, pack)
    return lax.cond(flag[0] > 2 * CAP, local_general, lambda *_: out, left, lpat, right, rpat)


def solution(mesh):
    placed = (
        P("row", ("layer", "col")),
        P("row", ("layer", "col")),
        P(("layer", "col"), "row"),
        P(("layer", "col"), "row"),
    )
    sizes = tuple(mesh.shape[axis] for axis in ("row", "col", "layer"))
    local = local_packed if sizes == (4, 2, 4) else local_general
    return jax.shard_map(
        local, mesh=mesh, in_specs=placed, out_specs=P("row", ("col", "layer")), check_vma=False
    )
```

```python
import functools

import jax
import jax.numpy as jnp
from jax import lax
from jax.experimental import pallas as pl
from jax.experimental.pallas import tpu as pltpu
from jax.sharding import PartitionSpec as P

MESH = pl.DeviceIdType.MESH
BLOCK = 64
CAP = 148
SPARE = 16
EDGES = (0, 10, 20, 30, 40, 50, 58, 66, 74)
CHUNKS = len(EDGES) - 1
READY = (3, 5, 7, 8)
LAG = 2


def from_behind(x, axis, by):
    size = lax.axis_size(axis)
    return lax.ppermute(x, axis, [(i, (i + by) % size) for i in range(size)])


def scatter_sum(partial_value):
    axes = ("col", "layer")
    size = lax.axis_size(axes)
    width = partial_value.shape[1] // size
    here = lax.axis_index("col") * lax.axis_size("layer") + lax.axis_index("layer")

    def share(owner):
        return lax.dynamic_slice_in_dim(partial_value, (owner % size) * width, width, 1)

    total = share(here)
    for away in range(1, size):
        total = total + from_behind(share(here + away), axes, away)
    return total


def apply_pattern(values, pattern):
    rows, cols = values.shape
    block = rows // pattern.shape[0]
    shaped = values.reshape(pattern.shape[0], block, pattern.shape[1], block)
    masked = shaped * pattern[:, None, :, None].astype(jnp.bfloat16)
    return masked.reshape(rows, cols)


def local_general(left_blocks, left_pattern, right_blocks, right_pattern):
    left = apply_pattern(left_blocks, left_pattern)
    right = apply_pattern(right_blocks, right_pattern)
    left_rows = left.shape[0]
    range_cols = right.shape[1]
    cycle_size = lax.axis_size("row")
    position = lax.axis_index("row")
    partial_value = jnp.zeros((left_rows, range_cols * cycle_size), jnp.float32)
    current = right
    for step in range(cycle_size):
        if step > 0:
            current = from_behind(current, "row", 1)
        owner = (position - step) % cycle_size
        piece = jnp.dot(left, current, preferred_element_type=jnp.float32)
        partial_value = lax.dynamic_update_slice_in_dim(partial_value, piece, owner * range_cols, 1)
    return scatter_sum(partial_value).astype(jnp.bfloat16)


def turn(tile):
    return jnp.concatenate([tile[:, BLOCK:], tile[:, :BLOCK]], axis=1)


def join(a, b):
    left = jnp.where(lax.broadcasted_iota(jnp.int32, (1, 128), 1) < BLOCK, 1.0, 0.0)
    return a * left.astype(jnp.bfloat16) + b * (1.0 - left).astype(jnp.bfloat16)


def prepare(pattern_ref, code_ref, pack_ref):
    cols, kblocks = pattern_ref.shape
    count = kblocks * cols
    per_strip = 2 * kblocks

    def iota(shape, axis):
        return lax.broadcasted_iota(jnp.int32, shape, axis)

    block = iota((cols, count), 1)
    choose = iota((cols, count), 0) == 2 * (block // per_strip) + block % 2
    mine = iota((kblocks, count), 0) == (iota((kblocks, count), 1) % per_strip) // 2
    spread = jnp.dot(pattern_ref[...].astype(jnp.float32), jnp.where(mine, 1.0, 0.0),
                     preferred_element_type=jnp.float32)
    present = jnp.sum(jnp.where(choose, spread, 0.0), axis=0, keepdims=True)
    before = jnp.where(iota((count, count), 0) < iota((count, count), 1), 1.0, 0.0)
    slot = jnp.dot(jnp.broadcast_to(present, (8, count)), before,
                   preferred_element_type=jnp.float32)[0:1].astype(jnp.int32)
    index = iota((1, count), 1)
    there = present > 0.5
    place = jnp.where(slot < CAP, slot, jnp.maximum(2 * CAP + SPARE - 1 - slot, CAP))
    same = place % 2 == index % 2

    eye = iota((count, count), 0) == iota((count, count), 1)
    column = jnp.sum(jnp.where(eye, jnp.where(there, place, -1).astype(jnp.float32), 0.0), axis=1, keepdims=True)
    hit = jnp.where(column.astype(jnp.int32) == iota((count, count), 1), 1.0, 0.0)
    source = jnp.sum(hit * iota((count, count), 0).astype(jnp.float32), axis=0, keepdims=True).astype(jnp.int32)
    used = jnp.sum(hit, axis=0, keepdims=True) > 0.5
    source = jnp.clip(source, 0, count - 1)
    level = source % 2 == index % 2

    total = jnp.sum(present, axis=1, keepdims=True)
    over = jnp.where(total > CAP + SPARE, 1.0, 0.0)
    for g in range(cols // 2 - 1):
        upto = jnp.sum(jnp.where(index < per_strip * (g + 1), present, 0.0), axis=1, keepdims=True)
        over = jnp.maximum(over, jnp.where(upto > 2 * EDGES[READY[g]], 1.0, 0.0))
    weight = jnp.broadcast_to(total + 4096.0 * over, (1, count)).astype(jnp.int32)

    def put(ref, row, value):
        ref[row:row + 1, :] = value[:, :128]
        ref[row + 1:row + 2, :] = value[:, 128:]

    tiles = (CAP + SPARE) // 2
    put(code_ref, 0, jnp.where(there, place // 2 + jnp.where(same, 0, tiles), 2 * tiles))
    put(code_ref, 2, weight)
    put(pack_ref, 0, jnp.where(used, source // 2 + jnp.where(level, 0, count // 2), count))
    for ref, row in ((code_ref, 4), (code_ref, 6), (pack_ref, 2), (pack_ref, 4), (pack_ref, 6)):
        put(ref, row, jnp.zeros((1, count), jnp.int32))


def kernel(left_ref, lpat_ref, right_ref, code_ref, pack_ref, out_ref, flag_ref,
           masked, tiled, held, spill, foreign, lent, current, wide, part, swapped, got, done,
           codes, other_codes, scalars, flags, flag_scalars,
           zsend, zrecv, xsend, xrecv, rsend, rrecv, fsend, frecv, csend, crecv, ssem, gsend, grecv,
           spill_send, spill_recv, lend_send, lend_recv):
    z = lax.axis_index("row")
    col = lax.axis_index("col")
    layer = lax.axis_index("layer")
    core = lax.rem(layer, 2)
    chip = col * 2 + lax.div(layer, 2)
    tiles, last, most = CAP // 2, CAP // 2 - SPARE // 2, CAP // 2 + SPARE // 2
    rows = left_ref.shape[0]
    quarter, eighth = rows // 4, rows // 8
    kblocks = right_ref.shape[0] // BLOCK
    strips = right_ref.shape[1] // 128

    def device(q, which):
        return (z, lax.div(q, 2), lax.rem(q, 2) * 2 + which)

    def other(i):
        return lax.rem(chip + i, 4)

    def on_line(i):
        return (lax.rem(z + i, 4), col, layer)

    partner = device(chip, 1 - core)
    above, below = (z + 1, col, layer), (z - 1, col, layer)
    has_above, has_below = z < 3, z > 0

    def remote(src, dst, send, recv, to):
        return pltpu.make_async_remote_copy(
            src_ref=src, dst_ref=dst, send_sem=send, recv_sem=recv, device_id=to, device_id_type=MESH)

    barrier = pltpu.get_barrier_semaphore()
    for to in [partner] + [on_line(i) for i in (1, 2, 3)] + [device(other(i), core) for i in (1, 2, 3)]:
        pl.semaphore_signal(barrier, inc=1, device_id=to, device_id_type=MESH)
    codes[z] = code_ref[...]

    def cut(k, carry):
        for m in range(strips):
            tile = right_ref[pl.ds(pl.multiple_of(k * BLOCK, BLOCK), BLOCK), m * 128:(m + 1) * 128]
            tiled[m * kblocks + k] = tile
            tiled[(strips + m) * kblocks + k] = turn(tile)
        return carry

    lax.fori_loop(0, kblocks, cut, 0, unroll=2)
    tiled[2 * strips * kblocks] = jnp.zeros((BLOCK, 128), jnp.bfloat16)
    current[2 * most] = jnp.zeros((BLOCK, 128), jnp.bfloat16)

    def packed(t):
        row, e = lax.div(t, 64), lax.rem(t, 64) * 2
        return join(tiled[pack_ref[row, e]], tiled[pack_ref[row, e + 1]])

    def pack(c):
        def one(t, carry):
            held[z, t] = packed(t)
            return carry

        def with_foreign(t, carry):
            held[z, t] = packed(t) + foreign[t - last]
            return carry
        lax.fori_loop(EDGES[c], EDGES[c + 1], one if c < CHUNKS - 1 else with_foreign, 0)

    def pack_spill(t, carry):
        spill[t] = packed(tiles + t)
        return carry

    def span(c):
        return pl.ds(EDGES[c], EDGES[c + 1] - EDGES[c])

    def lend(r):
        return remote(held.at[order(r), pl.ds(last, SPARE // 2)], lent.at[r], lend_send.at[r], lend_recv.at[r], partner)

    def up(j, c):
        piece = held.at[j, span(c)]
        return remote(piece, piece, zsend.at[0, j, c], zrecv.at[j, c], above)

    def down(j, c):
        piece = held.at[j, span(c)]
        return remote(piece, piece, zsend.at[1, j, c], zrecv.at[j, c], below)

    def tell(i):
        return remote(codes.at[z], codes.at[z], csend.at[i - 1], crecv.at[z], on_line(i))

    def told(i):
        j = lax.rem(z + i, 4)
        return remote(codes.at[j], codes.at[j], csend.at[i - 1], crecv.at[j], on_line(i))

    pack(0)
    pl.semaphore_wait(barrier, 7)
    for i in range(1, 4):
        tell(i).start()
    spilled = remote(spill, foreign, spill_send, spill_recv, partner)
    for c in range(CHUNKS):
        if c == CHUNKS - 1:
            spilled.wait_recv()
        if c > 0:
            pack(c)

        @pl.when(has_above)
        def _():
            up(z, c).start()

        @pl.when(has_below)
        def _():
            down(z, c).start()

        if c == 0:
            lax.fori_loop(0, SPARE // 2, pack_spill, 0)
            spilled.start()

    depth = left_ref.shape[1]
    spread = (lax.broadcasted_iota(jnp.int32, (depth // BLOCK, depth), 1) // BLOCK
              == lax.broadcasted_iota(jnp.int32, (depth // BLOCK, depth), 0))
    lmask = jnp.dot(lpat_ref[...].astype(jnp.float32), jnp.where(spread, 1.0, 0.0),
                    preferred_element_type=jnp.float32)
    for i in range(rows // BLOCK):
        masked[i * BLOCK:(i + 1) * BLOCK, :] = (
            left_ref[i * BLOCK:(i + 1) * BLOCK, :] * lmask[i:i + 1, :].astype(jnp.bfloat16))

    for i in range(1, 4):
        told(i).wait_recv()
    to_scalars = pltpu.make_async_copy(codes, scalars, ssem)
    to_scalars.start()
    to_scalars.wait()
    pair = remote(codes, other_codes, gsend.at[0], grecv.at[0], partner)
    pair.start()

    def spread_flag(i):
        return remote(flags.at[2], flags.at[6 - i], gsend.at[i], grecv.at[4 - i], device(other(i), core))

    def flag_from(i):
        return remote(flags.at[2], flags.at[2 + i], gsend.at[i], grecv.at[i], device(other(i), core))

    def order(r):
        y = jnp.where(z < 2, z, 3 - z)
        o = jnp.where(r == 0, y, jnp.where(r == 1, y + 1, jnp.where(r == 2, 2 - 2 * y, 3)))
        return jnp.where(z < 2, o, 3 - o)

    def step(r, c):
        @pl.when((r > 0) & (z + r <= 3))
        def _():
            j = z + r
            down(j, c).wait_recv()

            @pl.when(has_below)
            def _():
                down(j, c).start()

        @pl.when((r > 0) & (z - r >= 0))
        def _():
            j = z - r
            up(j, c).wait_recv()

            @pl.when(has_above)
            def _():
                up(j, c).start()

    def expand(r, g):
        j = order(r)

        def fetch(t, carry):
            current[t] = held[j, t]
            current[most + t] = turn(held[j, t])
            return carry
        first = 0 if g == 0 else READY[g - 1]
        if g == strips - 1:
            lend(r).start()
        lax.fori_loop(EDGES[first], EDGES[READY[g]], fetch, 0, unroll=2)
        if g == strips - 1:
            lend(r).wait_recv()
            for t in range(SPARE // 2):
                current[tiles + t] = lent[r, t]
                current[most + tiles + t] = turn(lent[r, t])

        def one(k, carry):
            row, e = g // 2, (g % 2) * 64 + 2 * k
            wide[pl.ds(pl.multiple_of(k * BLOCK, BLOCK), BLOCK), :] = join(
                current[scalars[j, row, e]], current[scalars[j, row, e + 1]])
            return carry
        lax.fori_loop(0, kblocks, one, 0, unroll=4)

    def swap(n, q):
        return remote(part.at[n, q, 1 - core], swapped.at[n, q], xsend.at[n, q], xrecv.at[n, q], partner)

    def multiply(n):
        def one(i, carry):
            pair = lax.rem(lax.div(chip, 2) + 1 + i, 2)
            piece = jnp.dot(masked[pl.ds(pl.multiple_of(pair * 2 * quarter, quarter), 2 * quarter), :], wide[...],
                            preferred_element_type=jnp.float32)
            for k in range(2):
                q = pair * 2 + k
                part[n, q, 0] = piece[2 * k * eighth:(2 * k + 1) * eighth]
                part[n, q, 1] = piece[(2 * k + 1) * eighth:(2 * k + 2) * eighth]
                swap(n, q).start()
            return carry
        lax.fori_loop(0, 2, one, 0)

    def scatter(n, i):
        return remote(part.at[n, other(i), core], got.at[n, 3 - i], rsend.at[n, i - 1], rrecv.at[n, 3 - i],
                      device(other(i), core))

    def arrival(n, i):
        return remote(part.at[n, chip, core], got.at[n, i - 1], rsend.at[n, i - 1], rrecv.at[n, i - 1],
                      device(other(i), core))

    def add_cores(n):
        for i in range(1, 5):
            q = other(i)
            swap(n, q).wait_recv()
            part[n, q, core] = part[n, q, core] + swapped[n, q]
            if i < 4:
                scatter(n, i).start()

    def deliver(n, to, which, place, source, source_core):
        rng = pl.ds(pl.multiple_of(source * quarter + source_core * eighth, eighth), eighth)
        return remote(done.at[n], out_ref.at[rng, pl.ds(pl.multiple_of(place * 128, 128), 128)],
                      fsend.at[n], frecv.at[place, source, source_core], device(to, which))

    def finish(n, r, g):
        j, which, place = order(r), g // 2, g % 2
        for i in range(1, 4):
            arrival(n, i).wait_recv()
        total = (part[n, chip, core] + got[n, 0]) + (got[n, 1] + got[n, 2])
        here = (j == chip) & (core == which)

        @pl.when(here)
        def _():
            rng = pl.ds(pl.multiple_of(chip * quarter + core * eighth, eighth), eighth)
            out_ref[rng, place * 128:(place + 1) * 128] = total.astype(jnp.bfloat16)

        @pl.when(jnp.logical_not(here))
        def _():
            done[n] = total.astype(jnp.bfloat16)
            deliver(n, j, which, place, chip, core).start()

    def rank(r, carry):
        for g in range(strips):
            n = r * strips + g
            for c in range(0 if g == 0 else READY[g - 1], READY[g]):
                step(r, c)
            expand(r, g)
            multiply(n)
            add_cores(n)
            if g >= LAG:
                finish(n - LAG, r, g - LAG)
            else:
                @pl.when(r > 0)
                def _():
                    finish(n - LAG, r - 1, strips + g - LAG)
        return carry

    pair.wait_recv()
    sums = [codes[j] + other_codes[j] for j in range(4)]
    flags[2] = jnp.maximum(jnp.maximum(sums[0], sums[1]), jnp.maximum(sums[2], sums[3]))
    for i in range(1, 4):
        spread_flag(i).start()
    lax.fori_loop(0, 4, rank, 0)
    for g in range(strips - LAG, strips):
        finish(3 * strips + g, 3, g)

    for i in range(1, 4):
        flag_from(i).wait_recv()
    flags[6] = jnp.maximum(jnp.maximum(flags[2], flags[3]), jnp.maximum(flags[4], flags[5]))
    to_flag = pltpu.make_async_copy(flags.at[6], flag_scalars, ssem)
    to_flag.start()
    to_flag.wait()
    flag_ref[0] = flag_scalars[2, 0]
    pair.wait_send()
    spilled.wait_send()
    for i in range(1, 4):
        spread_flag(i).wait_send()
        tell(i).wait_send()

    for place in range(2):
        for i in range(4):
            for source_core in range(2):
                @pl.when((i > 0) | (core != source_core))
                def _():
                    deliver(0, chip, core, place, other(i), source_core).wait_recv()

    def drain(r, carry):
        for g in range(strips):
            n = r * strips + g

            if g == 0:
                lend(r).wait_send()

            @pl.when((order(r) != chip) | (core != g // 2))
            def _():
                deliver(n, order(r), g // 2, g % 2, chip, core).wait_send()
            for q in range(4):
                swap(n, q).wait_send()
            for i in range(1, 4):
                scatter(n, i).wait_send()
        for c in range(CHUNKS):
            @pl.when(has_above & (r <= z))
            def _():
                up(r, c).wait_send()

            @pl.when(has_below & (r >= z))
            def _():
                down(r, c).wait_send()
        return carry

    lax.fori_loop(0, 4, drain, 0)


def run(left, lpat, right, code, pack):
    rows, width = left.shape[0], right.shape[1]
    eighth = rows // 8
    strips = width // 128
    units = 4 * strips
    dma = pltpu.SemaphoreType.DMA
    vmem = pl.BlockSpec(memory_space=pltpu.VMEM)
    smem = pl.BlockSpec(memory_space=pltpu.SMEM)
    tiles = (right.shape[0] // BLOCK) * strips
    return pl.pallas_call(
        kernel,
        out_shape=(jax.ShapeDtypeStruct((rows, width // 2), jnp.bfloat16),
                   jax.ShapeDtypeStruct((1,), jnp.int32)),
        in_specs=[vmem, vmem, vmem, vmem, smem],
        out_specs=(vmem, smem),
        scratch_shapes=[
            pltpu.VMEM(left.shape, jnp.bfloat16),
            pltpu.VMEM((2 * tiles + 1, BLOCK, 128), jnp.bfloat16),
            pltpu.VMEM((4, CAP // 2, BLOCK, 128), jnp.bfloat16),
            pltpu.VMEM((SPARE // 2, BLOCK, 128), jnp.bfloat16),
            pltpu.VMEM((SPARE // 2, BLOCK, 128), jnp.bfloat16),
            pltpu.VMEM((4, SPARE // 2, BLOCK, 128), jnp.bfloat16),
            pltpu.VMEM((CAP + SPARE + 1, BLOCK, 128), jnp.bfloat16),
            pltpu.VMEM((right.shape[0], 128), jnp.bfloat16),
            pltpu.VMEM((units, 4, 2, eighth, 128), jnp.float32),
            pltpu.VMEM((units, 4, eighth, 128), jnp.float32),
            pltpu.VMEM((units, 3, eighth, 128), jnp.float32),
            pltpu.VMEM((units, eighth, 128), jnp.bfloat16),
            pltpu.VMEM((4, 8, 128), jnp.int32),
            pltpu.VMEM((4, 8, 128), jnp.int32),
            pltpu.SMEM((4, 8, 128), jnp.int32),
            pltpu.VMEM((7, 8, 128), jnp.int32),
            pltpu.SMEM((8, 128), jnp.int32),
            dma((2, 4, CHUNKS)), dma((4, CHUNKS)),
            dma((units, 4)), dma((units, 4)), dma((units, 3)), dma((units, 3)),
            dma((units,)), dma((2, 4, 2)), dma((3,)), dma((4,)), dma, dma((4,)), dma((4,)),
            dma, dma, dma((4,)), dma((4,)),
        ],
        compiler_params=pltpu.CompilerParams(
            collective_id=0, has_side_effects=True, vmem_limit_bytes=56 * 2**20),
        name="sparse_product",
    )(left, lpat, right, code, pack)


def local_packed(left, lpat, right, rpat):
    table = jax.ShapeDtypeStruct((8, 128), jnp.int32)
    vmem = pl.BlockSpec(memory_space=pltpu.VMEM)
    code, pack = pl.pallas_call(
        prepare, out_shape=(table, table), in_specs=[vmem], out_specs=(vmem, vmem), name="places")(rpat.T)
    out, flag = run(left, lpat, right, code, pack)
    return lax.cond(flag[0] > 2 * CAP, local_general, lambda *_: out, left, lpat, right, rpat)


def solution(mesh):
    placed = (
        P("row", ("layer", "col")),
        P("row", ("layer", "col")),
        P(("layer", "col"), "row"),
        P(("layer", "col"), "row"),
    )
    sizes = tuple(mesh.shape[axis] for axis in ("row", "col", "layer"))
    local = local_packed if sizes == (4, 2, 4) else local_general
    return jax.shard_map(
        local, mesh=mesh, in_specs=placed, out_specs=P("row", ("col", "layer")), check_vma=False
    )
```

```python
import functools

import jax
import jax.numpy as jnp
from jax import lax
from jax.experimental import pallas as pl
from jax.experimental.pallas import tpu as pltpu
from jax.sharding import PartitionSpec as P

MESH = pl.DeviceIdType.MESH
BLOCK = 64
CAP = 148
SPARE = 16
EDGES = (0, 10, 20, 30, 40, 50, 56, 62, 66, 74)
CHUNKS = len(EDGES) - 1
READY = (3, 5, 7, 9)
LAG = 2


def from_behind(x, axis, by):
    size = lax.axis_size(axis)
    return lax.ppermute(x, axis, [(i, (i + by) % size) for i in range(size)])


def scatter_sum(partial_value):
    axes = ("col", "layer")
    size = lax.axis_size(axes)
    width = partial_value.shape[1] // size
    here = lax.axis_index("col") * lax.axis_size("layer") + lax.axis_index("layer")

    def share(owner):
        return lax.dynamic_slice_in_dim(partial_value, (owner % size) * width, width, 1)

    total = share(here)
    for away in range(1, size):
        total = total + from_behind(share(here + away), axes, away)
    return total


def apply_pattern(values, pattern):
    rows, cols = values.shape
    block = rows // pattern.shape[0]
    shaped = values.reshape(pattern.shape[0], block, pattern.shape[1], block)
    masked = shaped * pattern[:, None, :, None].astype(jnp.bfloat16)
    return masked.reshape(rows, cols)


def local_general(left_blocks, left_pattern, right_blocks, right_pattern):
    left = apply_pattern(left_blocks, left_pattern)
    right = apply_pattern(right_blocks, right_pattern)
    left_rows = left.shape[0]
    range_cols = right.shape[1]
    cycle_size = lax.axis_size("row")
    position = lax.axis_index("row")
    partial_value = jnp.zeros((left_rows, range_cols * cycle_size), jnp.float32)
    current = right
    for step in range(cycle_size):
        if step > 0:
            current = from_behind(current, "row", 1)
        owner = (position - step) % cycle_size
        piece = jnp.dot(left, current, preferred_element_type=jnp.float32)
        partial_value = lax.dynamic_update_slice_in_dim(partial_value, piece, owner * range_cols, 1)
    return scatter_sum(partial_value).astype(jnp.bfloat16)


def turn(tile):
    return jnp.concatenate([tile[:, BLOCK:], tile[:, :BLOCK]], axis=1)


def join(a, b):
    left = jnp.where(lax.broadcasted_iota(jnp.int32, (1, 128), 1) < BLOCK, 1.0, 0.0)
    return a * left.astype(jnp.bfloat16) + b * (1.0 - left).astype(jnp.bfloat16)


def prepare(pattern_ref, code_ref, pack_ref):
    cols, kblocks = pattern_ref.shape
    count = kblocks * cols
    per_strip = 2 * kblocks

    def iota(shape, axis):
        return lax.broadcasted_iota(jnp.int32, shape, axis)

    block = iota((cols, count), 1)
    choose = iota((cols, count), 0) == 2 * (block // per_strip) + block % 2
    mine = iota((kblocks, count), 0) == (iota((kblocks, count), 1) % per_strip) // 2
    spread = jnp.dot(pattern_ref[...].astype(jnp.float32), jnp.where(mine, 1.0, 0.0),
                     preferred_element_type=jnp.float32)
    present = jnp.sum(jnp.where(choose, spread, 0.0), axis=0, keepdims=True)
    before = jnp.where(iota((count, count), 0) < iota((count, count), 1), 1.0, 0.0)
    slot = jnp.dot(jnp.broadcast_to(present, (8, count)), before,
                   preferred_element_type=jnp.float32)[0:1].astype(jnp.int32)
    index = iota((1, count), 1)
    there = present > 0.5
    place = jnp.where(slot < CAP, slot, jnp.maximum(2 * CAP + SPARE - 1 - slot, CAP))
    same = place % 2 == index % 2

    eye = iota((count, count), 0) == iota((count, count), 1)
    column = jnp.sum(jnp.where(eye, jnp.where(there, place, -1).astype(jnp.float32), 0.0), axis=1, keepdims=True)
    hit = jnp.where(column.astype(jnp.int32) == iota((count, count), 1), 1.0, 0.0)
    source = jnp.sum(hit * iota((count, count), 0).astype(jnp.float32), axis=0, keepdims=True).astype(jnp.int32)
    used = jnp.sum(hit, axis=0, keepdims=True) > 0.5
    source = jnp.clip(source, 0, count - 1)
    level = source % 2 == index % 2

    total = jnp.sum(present, axis=1, keepdims=True)
    over = jnp.where(total > CAP + SPARE, 1.0, 0.0)
    for g in range(cols // 2 - 1):
        upto = jnp.sum(jnp.where(index < per_strip * (g + 1), present, 0.0), axis=1, keepdims=True)
        over = jnp.maximum(over, jnp.where(upto > 2 * EDGES[READY[g]], 1.0, 0.0))
    weight = jnp.broadcast_to(total + 4096.0 * over, (1, count)).astype(jnp.int32)

    def put(ref, row, value):
        ref[row:row + 1, :] = value[:, :128]
        ref[row + 1:row + 2, :] = value[:, 128:]

    tiles = (CAP + SPARE) // 2
    put(code_ref, 0, jnp.where(there, place // 2 + jnp.where(same, 0, tiles), 2 * tiles))
    put(code_ref, 2, weight)
    put(pack_ref, 0, jnp.where(used, source // 2 + jnp.where(level, 0, count // 2), count))
    for ref, row in ((code_ref, 4), (code_ref, 6), (pack_ref, 2), (pack_ref, 4), (pack_ref, 6)):
        put(ref, row, jnp.zeros((1, count), jnp.int32))


def kernel(left_ref, lpat_ref, right_ref, code_ref, pack_ref, out_ref, flag_ref,
           masked, tiled, held, spill, foreign, lent, current, wide, part, swapped, got, done,
           codes, other_codes, scalars, flags, flag_scalars,
           zsend, zrecv, xsend, xrecv, rsend, rrecv, fsend, frecv, csend, crecv, ssem, gsend, grecv,
           spill_send, spill_recv, lend_send, lend_recv):
    z = lax.axis_index("row")
    col = lax.axis_index("col")
    layer = lax.axis_index("layer")
    core = lax.rem(layer, 2)
    chip = col * 2 + lax.div(layer, 2)
    tiles, last, most = CAP // 2, CAP // 2 - SPARE // 2, CAP // 2 + SPARE // 2
    rows = left_ref.shape[0]
    quarter, eighth = rows // 4, rows // 8
    kblocks = right_ref.shape[0] // BLOCK
    strips = right_ref.shape[1] // 128

    def device(q, which):
        return (z, lax.div(q, 2), lax.rem(q, 2) * 2 + which)

    def other(i):
        return lax.rem(chip + i, 4)

    def on_line(i):
        return (lax.rem(z + i, 4), col, layer)

    partner = device(chip, 1 - core)
    above, below = (z + 1, col, layer), (z - 1, col, layer)
    has_above, has_below = z < 3, z > 0

    def remote(src, dst, send, recv, to):
        return pltpu.make_async_remote_copy(
            src_ref=src, dst_ref=dst, send_sem=send, recv_sem=recv, device_id=to, device_id_type=MESH)

    barrier = pltpu.get_barrier_semaphore()
    for to in [partner] + [on_line(i) for i in (1, 2, 3)] + [device(other(i), core) for i in (1, 2, 3)]:
        pl.semaphore_signal(barrier, inc=1, device_id=to, device_id_type=MESH)
    codes[z] = code_ref[...]

    def cut(k, carry):
        for m in range(strips):
            tile = right_ref[pl.ds(pl.multiple_of(k * BLOCK, BLOCK), BLOCK), m * 128:(m + 1) * 128]
            tiled[m * kblocks + k] = tile
            tiled[(strips + m) * kblocks + k] = turn(tile)
        return carry

    lax.fori_loop(0, kblocks, cut, 0, unroll=2)
    tiled[2 * strips * kblocks] = jnp.zeros((BLOCK, 128), jnp.bfloat16)
    current[2 * most] = jnp.zeros((BLOCK, 128), jnp.bfloat16)

    def packed(t):
        row, e = lax.div(t, 64), lax.rem(t, 64) * 2
        return join(tiled[pack_ref[row, e]], tiled[pack_ref[row, e + 1]])

    def pack(c):
        def one(t, carry):
            held[z, t] = packed(t)
            return carry

        def with_foreign(t, carry):
            held[z, t] = packed(t) + foreign[t - last]
            return carry
        lax.fori_loop(EDGES[c], EDGES[c + 1], one if c < CHUNKS - 1 else with_foreign, 0)

    def pack_spill(t, carry):
        spill[t] = packed(tiles + t)
        return carry

    def span(c):
        return pl.ds(EDGES[c], EDGES[c + 1] - EDGES[c])

    def lend(r):
        return remote(held.at[order(r), pl.ds(last, SPARE // 2)], lent.at[r], lend_send.at[r], lend_recv.at[r], partner)

    def up(j, c):
        piece = held.at[j, span(c)]
        return remote(piece, piece, zsend.at[0, j, c], zrecv.at[j, c], above)

    def down(j, c):
        piece = held.at[j, span(c)]
        return remote(piece, piece, zsend.at[1, j, c], zrecv.at[j, c], below)

    def tell(i):
        return remote(codes.at[z], codes.at[z], csend.at[i - 1], crecv.at[z], on_line(i))

    def told(i):
        j = lax.rem(z + i, 4)
        return remote(codes.at[j], codes.at[j], csend.at[i - 1], crecv.at[j], on_line(i))

    pack(0)
    pl.semaphore_wait(barrier, 7)
    for i in range(1, 4):
        tell(i).start()
    spilled = remote(spill, foreign, spill_send, spill_recv, partner)
    for c in range(CHUNKS):
        if c == CHUNKS - 1:
            spilled.wait_recv()
        if c > 0:
            pack(c)

        @pl.when(has_above)
        def _():
            up(z, c).start()

        @pl.when(has_below)
        def _():
            down(z, c).start()

        if c == 0:
            lax.fori_loop(0, SPARE // 2, pack_spill, 0)
            spilled.start()

    depth = left_ref.shape[1]
    spread = (lax.broadcasted_iota(jnp.int32, (depth // BLOCK, depth), 1) // BLOCK
              == lax.broadcasted_iota(jnp.int32, (depth // BLOCK, depth), 0))
    lmask = jnp.dot(lpat_ref[...].astype(jnp.float32), jnp.where(spread, 1.0, 0.0),
                    preferred_element_type=jnp.float32)
    for i in range(rows // BLOCK):
        masked[i * BLOCK:(i + 1) * BLOCK, :] = (
            left_ref[i * BLOCK:(i + 1) * BLOCK, :] * lmask[i:i + 1, :].astype(jnp.bfloat16))

    for i in range(1, 4):
        told(i).wait_recv()
    to_scalars = pltpu.make_async_copy(codes, scalars, ssem)
    to_scalars.start()
    to_scalars.wait()
    pair = remote(codes, other_codes, gsend.at[0], grecv.at[0], partner)
    pair.start()

    def spread_flag(i):
        return remote(flags.at[2], flags.at[6 - i], gsend.at[i], grecv.at[4 - i], device(other(i), core))

    def flag_from(i):
        return remote(flags.at[2], flags.at[2 + i], gsend.at[i], grecv.at[i], device(other(i), core))

    def order(r):
        y = jnp.where(z < 2, z, 3 - z)
        o = jnp.where(r == 0, y, jnp.where(r == 1, y + 1, jnp.where(r == 2, 2 - 2 * y, 3)))
        return jnp.where(z < 2, o, 3 - o)

    def step(r, c):
        @pl.when((r > 0) & (z + r <= 3))
        def _():
            j = z + r
            down(j, c).wait_recv()

            @pl.when(has_below)
            def _():
                down(j, c).start()

        @pl.when((r > 0) & (z - r >= 0))
        def _():
            j = z - r
            up(j, c).wait_recv()

            @pl.when(has_above)
            def _():
                up(j, c).start()

    def expand(r, g):
        j = order(r)

        def fetch(t, carry):
            current[t] = held[j, t]
            current[most + t] = turn(held[j, t])
            return carry
        first = 0 if g == 0 else READY[g - 1]
        if g == strips - 1:
            lend(r).start()
        lax.fori_loop(EDGES[first], EDGES[READY[g]], fetch, 0, unroll=2)
        if g == strips - 1:
            lend(r).wait_recv()
            for t in range(SPARE // 2):
                current[tiles + t] = lent[r, t]
                current[most + tiles + t] = turn(lent[r, t])

        def one(k, carry):
            row, e = g // 2, (g % 2) * 64 + 2 * k
            wide[pl.ds(pl.multiple_of(k * BLOCK, BLOCK), BLOCK), :] = join(
                current[scalars[j, row, e]], current[scalars[j, row, e + 1]])
            return carry
        lax.fori_loop(0, kblocks, one, 0, unroll=4)

    def swap(n, q):
        return remote(part.at[n, q, 1 - core], swapped.at[n, q], xsend.at[n, q], xrecv.at[n, q], partner)

    def multiply(n):
        def one(i, carry):
            pair = lax.rem(lax.div(chip, 2) + 1 + i, 2)
            piece = jnp.dot(masked[pl.ds(pl.multiple_of(pair * 2 * quarter, quarter), 2 * quarter), :], wide[...],
                            preferred_element_type=jnp.float32)
            for k in range(2):
                q = pair * 2 + k
                part[n, q, 0] = piece[2 * k * eighth:(2 * k + 1) * eighth]
                part[n, q, 1] = piece[(2 * k + 1) * eighth:(2 * k + 2) * eighth]
                swap(n, q).start()
            return carry
        lax.fori_loop(0, 2, one, 0)

    def scatter(n, i):
        return remote(part.at[n, other(i), core], got.at[n, 3 - i], rsend.at[n, i - 1], rrecv.at[n, 3 - i],
                      device(other(i), core))

    def arrival(n, i):
        return remote(part.at[n, chip, core], got.at[n, i - 1], rsend.at[n, i - 1], rrecv.at[n, i - 1],
                      device(other(i), core))

    def add_cores(n):
        for k in range(1, 5):
            i = jnp.where(lax.rem(chip, 2) == 1, k, k % 3 + 1) if k < 4 else 4
            q = other(i)
            swap(n, q).wait_recv()
            part[n, q, core] = part[n, q, core] + swapped[n, q]
            if k < 4:
                scatter(n, i).start()

    def deliver(n, to, which, place, source, source_core):
        rng = pl.ds(pl.multiple_of(source * quarter + source_core * eighth, eighth), eighth)
        return remote(done.at[n], out_ref.at[rng, pl.ds(pl.multiple_of(place * 128, 128), 128)],
                      fsend.at[n], frecv.at[place, source, source_core], device(to, which))

    def finish(n, r, g):
        j, which, place = order(r), g // 2, g % 2
        for i in range(1, 4):
            arrival(n, i).wait_recv()
        total = (part[n, chip, core] + got[n, 0]) + (got[n, 1] + got[n, 2])
        here = (j == chip) & (core == which)

        @pl.when(here)
        def _():
            rng = pl.ds(pl.multiple_of(chip * quarter + core * eighth, eighth), eighth)
            out_ref[rng, place * 128:(place + 1) * 128] = total.astype(jnp.bfloat16)

        @pl.when(jnp.logical_not(here))
        def _():
            done[n] = total.astype(jnp.bfloat16)
            deliver(n, j, which, place, chip, core).start()

    def rank(r, carry):
        for g in range(strips):
            n = r * strips + g
            for c in range(0 if g == 0 else READY[g - 1], READY[g]):
                step(r, c)
            expand(r, g)
            multiply(n)
            add_cores(n)
            if g >= LAG:
                finish(n - LAG, r, g - LAG)
            else:
                @pl.when(r > 0)
                def _():
                    finish(n - LAG, r - 1, strips + g - LAG)
        return carry

    pair.wait_recv()
    sums = [codes[j] + other_codes[j] for j in range(4)]
    flags[2] = jnp.maximum(jnp.maximum(sums[0], sums[1]), jnp.maximum(sums[2], sums[3]))
    for i in range(1, 4):
        spread_flag(i).start()
    lax.fori_loop(0, 4, rank, 0)
    for g in range(strips - LAG, strips):
        finish(3 * strips + g, 3, g)

    for i in range(1, 4):
        flag_from(i).wait_recv()
    flags[6] = jnp.maximum(jnp.maximum(flags[2], flags[3]), jnp.maximum(flags[4], flags[5]))
    to_flag = pltpu.make_async_copy(flags.at[6], flag_scalars, ssem)
    to_flag.start()
    to_flag.wait()
    flag_ref[0] = flag_scalars[2, 0]
    pair.wait_send()
    spilled.wait_send()
    for i in range(1, 4):
        spread_flag(i).wait_send()
        tell(i).wait_send()

    for place in range(2):
        for i in range(4):
            for source_core in range(2):
                @pl.when((i > 0) | (core != source_core))
                def _():
                    deliver(0, chip, core, place, other(i), source_core).wait_recv()

    def drain(r, carry):
        for g in range(strips):
            n = r * strips + g

            if g == 0:
                lend(r).wait_send()

            @pl.when((order(r) != chip) | (core != g // 2))
            def _():
                deliver(n, order(r), g // 2, g % 2, chip, core).wait_send()
            for q in range(4):
                swap(n, q).wait_send()
            for i in range(1, 4):
                scatter(n, i).wait_send()
        for c in range(CHUNKS):
            @pl.when(has_above & (r <= z))
            def _():
                up(r, c).wait_send()

            @pl.when(has_below & (r >= z))
            def _():
                down(r, c).wait_send()
        return carry

    lax.fori_loop(0, 4, drain, 0)


def run(left, lpat, right, code, pack):
    rows, width = left.shape[0], right.shape[1]
    eighth = rows // 8
    strips = width // 128
    units = 4 * strips
    dma = pltpu.SemaphoreType.DMA
    vmem = pl.BlockSpec(memory_space=pltpu.VMEM)
    smem = pl.BlockSpec(memory_space=pltpu.SMEM)
    tiles = (right.shape[0] // BLOCK) * strips
    return pl.pallas_call(
        kernel,
        out_shape=(jax.ShapeDtypeStruct((rows, width // 2), jnp.bfloat16),
                   jax.ShapeDtypeStruct((1,), jnp.int32)),
        in_specs=[vmem, vmem, vmem, vmem, smem],
        out_specs=(vmem, smem),
        scratch_shapes=[
            pltpu.VMEM(left.shape, jnp.bfloat16),
            pltpu.VMEM((2 * tiles + 1, BLOCK, 128), jnp.bfloat16),
            pltpu.VMEM((4, CAP // 2, BLOCK, 128), jnp.bfloat16),
            pltpu.VMEM((SPARE // 2, BLOCK, 128), jnp.bfloat16),
            pltpu.VMEM((SPARE // 2, BLOCK, 128), jnp.bfloat16),
            pltpu.VMEM((4, SPARE // 2, BLOCK, 128), jnp.bfloat16),
            pltpu.VMEM((CAP + SPARE + 1, BLOCK, 128), jnp.bfloat16),
            pltpu.VMEM((right.shape[0], 128), jnp.bfloat16),
            pltpu.VMEM((units, 4, 2, eighth, 128), jnp.float32),
            pltpu.VMEM((units, 4, eighth, 128), jnp.float32),
            pltpu.VMEM((units, 3, eighth, 128), jnp.float32),
            pltpu.VMEM((units, eighth, 128), jnp.bfloat16),
            pltpu.VMEM((4, 8, 128), jnp.int32),
            pltpu.VMEM((4, 8, 128), jnp.int32),
            pltpu.SMEM((4, 8, 128), jnp.int32),
            pltpu.VMEM((7, 8, 128), jnp.int32),
            pltpu.SMEM((8, 128), jnp.int32),
            dma((2, 4, CHUNKS)), dma((4, CHUNKS)),
            dma((units, 4)), dma((units, 4)), dma((units, 3)), dma((units, 3)),
            dma((units,)), dma((2, 4, 2)), dma((3,)), dma((4,)), dma, dma((4,)), dma((4,)),
            dma, dma, dma((4,)), dma((4,)),
        ],
        compiler_params=pltpu.CompilerParams(
            collective_id=0, has_side_effects=True, vmem_limit_bytes=56 * 2**20),
        name="sparse_product",
    )(left, lpat, right, code, pack)


def local_packed(left, lpat, right, rpat):
    table = jax.ShapeDtypeStruct((8, 128), jnp.int32)
    vmem = pl.BlockSpec(memory_space=pltpu.VMEM)
    code, pack = pl.pallas_call(
        prepare, out_shape=(table, table), in_specs=[vmem], out_specs=(vmem, vmem), name="places")(rpat.T)
    out, flag = run(left, lpat, right, code, pack)
    return lax.cond(flag[0] > 2 * CAP, local_general, lambda *_: out, left, lpat, right, rpat)


def solution(mesh):
    placed = (
        P("row", ("layer", "col")),
        P("row", ("layer", "col")),
        P(("layer", "col"), "row"),
        P(("layer", "col"), "row"),
    )
    sizes = tuple(mesh.shape[axis] for axis in ("row", "col", "layer"))
    local = local_packed if sizes == (4, 2, 4) else local_general
    return jax.shard_map(
        local, mesh=mesh, in_specs=placed, out_specs=P("row", ("col", "layer")), check_vma=False
    )
```
